32 devices in a mesh: shard: 8 (over z, x), tensor: 4 (over y, core).
Axes of the slice: x: 2, y: 2, z: 4, core: 2. Of those that a mesh axis runs over, the one named last changes fastest.
Arguments:
- hidden_acts: bfloat16 [2, 2048, 10944], P(None, 'shard', 'tensor'), may hold values from -18 to 18
- out_grads: bfloat16 [2, 2048, 1024], P(None, 'shard'), may hold values from -18 to 18
- sample_idx: int32 [2, 1024], P(None, 'shard'), may hold values from 0 to 255
- grad_weight: bfloat16 [1024, 10944], P('shard', 'tensor'), may hold values from -112 to 112
- momentum: float32 [1024, 10944], P('shard', 'tensor'), may hold values from -6 to 6
- weight: float32 [1024, 10944], P('shard', 'tensor'), may hold values from -6 to 6
Outputs:
- new_momentum: float32 [1024, 10944], P('shard', 'tensor')
- new_weight: float32 [1024, 10944], P('shard', 'tensor')
The draws below stay inside these ranges and needn't reach their ends.
All inputs are finite; a program needn't handle non-finite values.
Results may differ from the reference program's by a relative error of at most 0.0085.
Values may be sent and summed in bfloat16 or wider, within the bound.
No kernel may reach another device: no remote copies, remote signals or barrier semaphores. Data moves between devices by JAX's collectives and lax.ppermute only.
A program may use at most 128 MiB of HBM per device.

```python
import math
import jax
import jax.numpy as jnp
from jax import lax

DOUT = 1024
FF = 10944
ABLK = 1368
NS_STEPS = 2
MBATCH = 2
TOK_DEV = 256
SAMP = 128
TOKENS = 2048
SAMPLES = 1024
N_SHARD = 8


def log_spread(key, count, low, high):
    return jnp.exp(jax.random.uniform(key, (count,), jnp.float32, math.log(low), math.log(high)))


def feature_draw(key, width, latent):
    keys = jax.random.split(key, 7)
    ngroups = TOKENS // TOK_DEV
    token_scale = log_spread(keys[1], MBATCH * TOKENS, 0.5, 2.0).reshape(MBATCH, TOKENS, 1)
    group_cols = log_spread(keys[2], ngroups * width, 0.3, 3.0).reshape(ngroups, width)
    sources = jax.random.randint(keys[4], (4, width), 0, latent)
    signs = (2 * jax.random.randint(keys[5], (4, width), 0, 2) - 1).astype(jnp.float32)
    weights = jax.random.uniform(keys[6], (4, width), jnp.float32, 0.5, 1.0) * signs
    rise = 10.0
    latents = jax.random.truncated_normal(keys[0], -4.0, 4.0, (MBATCH, TOKENS, latent), jnp.float32)
    own = jax.random.truncated_normal(keys[3], -4.0, 4.0, (MBATCH, TOKENS, width), jnp.float32)
    base = 0.5 * own
    for term in range(4):
        base = base + weights[term] * jnp.take(latents, sources[term], axis=2)
    base = 0.5 * base
    base = jnp.clip(base, -3.0, 3.0)
    base = base * token_scale
    group_pos = jnp.arange(ngroups, dtype=jnp.float32) / max(ngroups - 1, 1)
    group_scale = jnp.sqrt((1.0 + (rise - 1.0) * group_pos) / rise)
    factor = group_cols * group_scale[:, None]
    shaped = base.reshape(MBATCH, ngroups, TOK_DEV, width) * factor[None, :, None, :]
    return shaped.reshape(MBATCH, TOKENS, width).astype(jnp.bfloat16)


def draw_hidden_acts(key, part):
    return feature_draw(jax.random.fold_in(key, 3), FF, FF // 4)


def draw_out_grads(key, part):
    return feature_draw(jax.random.fold_in(key, 7), DOUT, DOUT // 2)


def draw_grad_weight(key, part):
    keys = jax.random.split(jax.random.fold_in(key, 11), 3)
    row_pos = jnp.arange(DOUT, dtype=jnp.float32) / DOUT
    col_pos = jnp.arange(FF, dtype=jnp.float32) / FF
    rise = 2.0
    base = jax.random.truncated_normal(keys[0], -4.0, 4.0, (DOUT, FF), jnp.float32)
    row_scale = log_spread(keys[1], DOUT, 0.1, 1.0) * jnp.sqrt(1.0 + rise * row_pos)
    col_scale = log_spread(keys[2], FF, 0.3, 3.0) * jnp.sqrt(1.0 + rise * col_pos)
    return (base * row_scale[:, None] * col_scale[None, :]).astype(jnp.bfloat16)


def touch_ends(array, key, low, high):
    index_at = [jax.random.randint(jax.random.fold_in(key, axis), (), 0, length) for axis, length in enumerate(array.shape)]
    widest = array.shape.index(max(array.shape))
    neighbour = index_at[:widest] + [(index_at[widest] + 1) % array.shape[widest]] + index_at[widest + 1:]
    return array.at[tuple(index_at)].set(low).at[tuple(neighbour)].set(high)


def level_of(own_key, shape, cuts, least, high):
    factor_of = 1.0
    for axis_at, shards_of in cuts:
        draws = jax.random.uniform(jax.random.fold_in(jax.random.fold_in(own_key, 6), axis_at), (shards_of,), jnp.float32, least / len(cuts), high / len(cuts))
        factor_of = factor_of * jnp.repeat(jnp.exp(draws), shape[axis_at] // shards_of).reshape((-1,) + (1,) * (len(shape) - 1 - axis_at))
    return factor_of


def centred(rng, dims, spread, limit, shards=(), kind=jnp.bfloat16):
    values = jax.random.normal(rng, dims, jnp.float32) * spread
    if len(shards) > 0:
        values = level_of(rng, dims, shards, -0.22, 0.18) * values
    return jnp.clip(values, min=-limit, max=limit).astype(kind)


def setup_inputs(seed: int = 0) -> dict:
    key_of = jax.random.split(jax.random.key(seed), 7)
    return {
        "hidden_acts": draw_hidden_acts(jax.random.fold_in(key_of[6], 71), 0),
        "out_grads": draw_out_grads(jax.random.fold_in(key_of[6], 71), 0),
        "sample_idx": touch_ends(jax.random.randint(key_of[2], (MBATCH, SAMPLES), 0, TOK_DEV), jax.random.fold_in(key_of[2], 1), 0, TOK_DEV - 1).astype(jnp.int32),
        "grad_weight": draw_grad_weight(jax.random.fold_in(key_of[6], 71), 0),
        "momentum": centred(key_of[4], (DOUT, FF), 1.0, 6.0, ((0, 8), (1, 4)), jnp.float32),
        "weight": centred(key_of[5], (DOUT, FF), 0.5, 6.0, ((0, 8), (1, 4)), jnp.float32),
    }


DAMPING = 0.1
CLIP_LEVEL = 0.5
MOMENTUM_RATE = 0.9
LEARN_RATE = 0.5

def round_bf16(value):
    return lax.optimization_barrier(value.astype(jnp.bfloat16)).astype(jnp.float32)

def block_moments(rows, width, scale):
    stacked = rows.astype(jnp.float32).reshape(rows.shape[0], rows.shape[1] // width, width)
    moments = jnp.einsum('nkb,nkc->kbc', stacked, stacked)
    return round_bf16(moments * scale)

def newton_inverse(stat):
    width = stat.shape[0]
    shift = DAMPING * jnp.trace(stat) / width
    damped = stat + shift * jnp.eye(width, dtype=jnp.float32)
    normed = (damped / jnp.sqrt(jnp.sum(damped * damped))).astype(jnp.bfloat16)
    iterate = jnp.eye(width, dtype=jnp.bfloat16)
    for step in range(NS_STEPS):
        product = jnp.dot(normed, iterate, preferred_element_type=jnp.float32).astype(jnp.bfloat16)
        twice = 2.0 * iterate.astype(jnp.float32)
        iterate = (twice - jnp.dot(iterate, product, preferred_element_type=jnp.float32)).astype(jnp.bfloat16)
    return iterate

def reference(hidden_acts, out_grads, sample_idx, grad_weight, momentum, weight):
    scale = 1.0 / (MBATCH * SAMPLES)
    index = sample_idx.reshape(MBATCH, N_SHARD, SAMP)
    acts = hidden_acts.reshape(MBATCH, N_SHARD, TOK_DEV, FF)
    grads = out_grads.reshape(MBATCH, N_SHARD, TOK_DEV, DOUT)
    select = jax.vmap(jax.vmap(lambda tokens, where: jnp.take(tokens, where, axis=0)))
    picked_acts = jnp.transpose(select(acts, index), (1, 0, 2, 3))
    picked_grads = jnp.transpose(select(grads, index), (1, 0, 2, 3))

    def add_group(carry, group):
        act_sum, grad_sum = carry
        group_acts, group_grads = group
        act_rows = group_acts.reshape(MBATCH * SAMP, FF)
        grad_rows = group_grads.reshape(MBATCH * SAMP, DOUT)
        act_sum = act_sum + block_moments(act_rows, ABLK, scale)
        grad_sum = grad_sum + block_moments(grad_rows, DOUT, scale)
        return ((act_sum, grad_sum), None)
    start = (jnp.zeros((FF // ABLK, ABLK, ABLK), jnp.float32), jnp.zeros((1, DOUT, DOUT), jnp.float32))
    (act_stat, grad_stat), unused = lax.scan(add_group, start, (picked_acts, picked_grads))
    act_stat = round_bf16(act_stat)
    grad_stat = round_bf16(grad_stat)
    act_inverse = lax.map(newton_inverse, act_stat)
    grad_inverse = newton_inverse(grad_stat[0])
    left = jnp.dot(grad_inverse, grad_weight, preferred_element_type=jnp.float32).astype(jnp.bfloat16)
    left_blocks = left.astype(jnp.float32).reshape(DOUT, FF // ABLK, ABLK)
    update = jnp.einsum('rkb,kbc->rkc', left_blocks, act_inverse.astype(jnp.float32)).reshape(DOUT, FF)
    alignment = jnp.sum(update * grad_weight.astype(jnp.float32))
    ratio = jnp.minimum(1.0, CLIP_LEVEL / jnp.sqrt(alignment / (DOUT * FF)))
    new_momentum = MOMENTUM_RATE * momentum + ratio * update
    new_weight = weight - LEARN_RATE * new_momentum
    return (new_momentum, new_weight)
```

```python
import jax
import jax.numpy as jnp
from jax import lax
from jax.sharding import PartitionSpec as P

DOUT = 1024
FF = 10944
ABLK = 1368

DAMPING = 0.1
CLIP_LEVEL = 0.5
MOMENTUM_RATE = 0.9
LEARN_RATE = 0.5

AXES = ("shard", "tensor")


def permute(value, shards, tensors, target):
    pairs = []
    for s in range(shards):
        for t in range(tensors):
            to_s, to_t = target(s, t)
            pairs.append((s * tensors + t, to_s * tensors + to_t))
    return lax.ppermute(value, AXES, pairs)


def pick(tokens, where):
    hot = (where[:, None] == lax.broadcasted_iota(jnp.int32, (where.shape[0], tokens.shape[0]), 1))
    return jnp.dot(hot.astype(jnp.bfloat16), tokens, preferred_element_type=jnp.float32).astype(
        jnp.bfloat16
    )


def pick_transposed(tokens_t, where):
    hot = (where[None, :] == lax.broadcasted_iota(jnp.int32, (tokens_t.shape[1], where.shape[0]), 0))
    return jnp.dot(tokens_t, hot.astype(jnp.bfloat16), preferred_element_type=jnp.float32).astype(
        jnp.bfloat16
    )


def damping_terms(gram):
    width = gram.shape[0]
    trace = jnp.trace(gram)
    shift = DAMPING * trace / width
    total = jnp.sum(gram * gram) + 2.0 * shift * trace + width * shift * shift
    scale = 1.0 / jnp.sqrt(total)
    return scale, shift * scale


def dot_f32(a, b):
    return jnp.dot(a, b, preferred_element_type=jnp.float32)


def per_device(hidden_acts, out_grads, sample_idx, grad_weight, momentum, weight):
    n = lax.axis_size("shard")
    nt = lax.axis_size("tensor")
    batches, picks = sample_idx.shape
    rows, hidden = grad_weight.shape
    blocks = hidden // ABLK
    high = 2 * blocks
    m = n // high
    me = lax.axis_index("shard")
    col = lax.axis_index("tensor")
    core = col % 2
    hi = me // m
    lo = me % m

    def split(s, t):
        return s // m, s % m, t // 2, t % 2

    def send(value, f):
        def target(s, t):
            a, b, y, c = f(*split(s, t))
            return a * m + b, y * 2 + c

        return permute(value, n, nt, target)

    def over_lo(value, d):
        return send(value, lambda h, l, y, c: (h, l ^ d, y, c))

    def over_core(value):
        return send(value, lambda h, l, y, c: (h, l, y, c ^ 1))

    grad_t = grad_weight.T.reshape(blocks, ABLK, rows)
    home = lambda k: (lambda h, l, y, c: (2 * c + ((h ^ k) & 1), l, y, h >> 1))
    w_own = [
        send(lax.dynamic_index_in_dim(grad_t, (hi ^ k) & 1, 0, keepdims=False), home(k))
        for k in range(2)
    ]

    q_rows = batches * picks // nt
    flat_idx = sample_idx.reshape(-1)
    my_idx = lax.dynamic_slice_in_dim(flat_idx, col * q_rows, q_rows, 0)
    my_tokens = lax.dynamic_index_in_dim(
        out_grads, col * q_rows // picks, 0, keepdims=False
    )
    q = pick(my_tokens, my_idx)
    q = [q] + [
        send(q, lambda h, l, y, c, d=d: (h ^ d, l, y, c)) for d in range(1, high)
    ]
    q = jnp.concatenate(q, axis=0)

    acts_t = jnp.swapaxes(hidden_acts, 1, 2)
    picked = jnp.stack([pick_transposed(acts_t[i], sample_idx[i]) for i in range(batches)])
    picked = jnp.swapaxes(picked.reshape(batches, blocks, ABLK, picks), 0, 1)
    picked = picked.reshape(blocks * batches, ABLK, picks)
    spread = lambda k: (lambda h, l, y, c: (blocks * c + ((h ^ k) >> 1), l, y, (h ^ k) & 1))
    z_own = [
        send(lax.dynamic_index_in_dim(picked, hi ^ k, 0, keepdims=False), spread(k))
        for k in range(high)
    ]

    w_lo = w_own + [over_lo(w, d) for d in range(1, m) for w in w_own]
    w_all = w_lo + [over_core(w) for w in w_lo]

    q = jnp.concatenate([q] + [over_lo(q, d) for d in range(1, m)], axis=0)
    for step in range(1, nt // 2):
        pass
    others = [q]
    for d in range(1, nt // 2):
        others.append(send(q, lambda h, l, y, c, d=d: (h, l, y ^ d, c)))
    q = jnp.concatenate(others, axis=0)
    q = jnp.concatenate([q, over_core(q)], axis=0)

    z_lo = z_own + [over_lo(z, d) for d in range(1, m) for z in z_own]
    z_all = jnp.concatenate(z_lo + [over_core(z) for z in z_lo], axis=1)

    count = batches * picks * n
    g_gram = lax.dot_general(
        q, q, (((0,), (0,)), ((), ())), preferred_element_type=jnp.float32
    ) * (1.0 / count)
    g_scale, g_shift = damping_terms(g_gram)
    first = (2 * core + (hi & 1)) * m + lo
    mine = jnp.concatenate(
        [lax.dynamic_slice_in_dim(g_gram, (first ^ (k * m)) * rows, rows, 1) for k in range(2)],
        axis=1,
    )
    place = jnp.concatenate([(first ^ (k * m)) * rows + jnp.arange(rows) for k in range(2)])
    eye = (lax.broadcasted_iota(jnp.int32, (DOUT, 2 * rows), 0) == place[None, :])
    g_damped = g_gram * g_scale + g_shift * jnp.eye(DOUT, dtype=jnp.float32)
    g_norm = g_damped.astype(jnp.bfloat16)
    y1 = mine * g_scale + jnp.where(eye, g_shift, 0.0)
    y2 = dot_f32(g_norm, y1.astype(jnp.bfloat16))
    y3 = dot_f32(g_norm, y2.astype(jnp.bfloat16))
    g_poly = (4.0 * y2 - 6.0 * y1 - y3).astype(jnp.bfloat16).reshape(n, rows, 2 * rows)
    g_poly = jnp.concatenate(
        [lax.dynamic_index_in_dim(g_poly, first ^ r, 0, keepdims=False) for r in
         [dq * 2 * m + k * m + d for dq in range(2) for d in range(m) for k in range(2)]],
        axis=0,
    )
    w_mine = jnp.concatenate(w_own, axis=1).astype(jnp.float32)
    left = 4.0 * w_mine + dot_f32(jnp.concatenate(w_all, axis=1), g_poly)
    left = left.astype(jnp.bfloat16)

    a_gram = lax.dot_general(
        z_all, z_all, (((1,), (1,)), ((), ())), preferred_element_type=jnp.float32
    ) * (1.0 / count)
    a_scale, a_shift = damping_terms(a_gram)
    a_norm = (a_gram * a_scale + a_shift * jnp.eye(ABLK, dtype=jnp.float32)).astype(jnp.bfloat16)
    left_f = left.astype(jnp.float32)
    t1 = 4.0 * left_f - dot_f32(a_norm, left)
    t2 = dot_f32(a_norm, t1.astype(jnp.bfloat16)) - 6.0 * left_f
    update = dot_f32(a_norm, t2.astype(jnp.bfloat16)) + 4.0 * left_f

    total = jnp.sum(update * w_mine).reshape(1, 1)
    sent = update.astype(jnp.bfloat16)
    back = [send(sent[:, k * rows : (k + 1) * rows], home(k)) for k in range(2)]
    total = total + over_core(total)
    for d in [2**i for i in range(10) if 2**i < nt // 2]:
        total = total + send(total, lambda h, l, y, c, d=d: (h, l, y ^ d, c))
    for d in [2**i for i in range(10) if 2**i < m]:
        total = total + over_lo(total, d)
    for d in [2**i for i in range(10) if 2**i < high]:
        total = total + send(total, lambda h, l, y, c, d=d: (h ^ d, l, y, c))
    ratio = jnp.minimum(1.0, CLIP_LEVEL / jnp.sqrt(total[0, 0] / (DOUT * FF)))

    odd = (hi & 1) == 1
    final = jnp.concatenate(
        [jnp.where(odd, back[1 - j], back[j]) for j in range(2)], axis=0
    ).astype(jnp.float32)
    new_momentum = MOMENTUM_RATE * momentum.T + ratio * final
    new_weight = weight.T - LEARN_RATE * new_momentum
    return (new_momentum.T, new_weight.T)


def solution(mesh):
    in_specs = (
        P(None, "shard", "tensor"),
        P(None, "shard", None),
        P(None, "shard"),
        P("shard", "tensor"),
        P("shard", "tensor"),
        P("shard", "tensor"),
    )
    out_specs = (P("shard", "tensor"), P("shard", "tensor"))
    return jax.shard_map(
        per_device, mesh=mesh, in_specs=in_specs, out_specs=out_specs, check_vma=False
    )
```

```python
import functools

import jax
import jax.numpy as jnp
from jax import lax
from jax.experimental import pallas as pl
from jax.experimental.pallas import tpu as pltpu
from jax.sharding import PartitionSpec as P

DOUT = 1024
FF = 10944
ABLK = 1368

DAMPING = 0.1
CLIP_LEVEL = 0.5
MOMENTUM_RATE = 0.9
LEARN_RATE = 0.5

AXES = ("shard", "tensor")


def route(shards, tensors, target):
    pairs = []
    for s in range(shards):
        for t in range(tensors):
            to = target(s, t)
            if to is not None:
                pairs.append((s * tensors + t, to[0] * tensors + to[1]))
    return pairs


def pick(tokens, where):
    hot = (where[:, None] == lax.broadcasted_iota(jnp.int32, (where.shape[0], tokens.shape[0]), 1))
    return jnp.dot(hot.astype(jnp.bfloat16), tokens, preferred_element_type=jnp.float32).astype(
        jnp.bfloat16
    )


def pick_transposed(tokens_t, where):
    hot = (where[None, :] == lax.broadcasted_iota(jnp.int32, (tokens_t.shape[1], where.shape[0]), 0))
    return jnp.dot(tokens_t, hot.astype(jnp.bfloat16), preferred_element_type=jnp.float32).astype(
        jnp.bfloat16
    )


def row_tiles(width, limit):
    count = -(-width // limit)
    size = -(-width // (count * 16)) * 16
    return [(at, min(size, width - at)) for at in range(0, width, size)]


def dot_nt(a, b):
    return lax.dot_general(a, b, (((1,), (1,)), ((), ())), preferred_element_type=jnp.float32)


def dot_nn(a, b):
    return jnp.dot(a, b, preferred_element_type=jnp.float32)


def damping_terms(trace, squares, width):
    shift = DAMPING * trace / width
    norm = jnp.sqrt(squares + 2.0 * shift * trace + width * shift * shift)
    return 1.0 / norm, shift / norm


def lay_out(parts, wide):
    at = 0
    for part in parts:
        count, _, lanes = part.shape
        for i in range(count):
            wide[:, at : at + lanes] = part[i]
            at += lanes


def gram_kernel(*refs):
    *parts, out, wide = refs
    lay_out(parts, wide)
    for at, size in row_tiles(out.shape[0], 352):
        out[at : at + size, :] = dot_nt(wide[at : at + size, :], wide[...])


def factor_gram(wide, base, gram, scale):
    width = gram.shape[0]
    trace, squares = 0.0, 0.0
    for at, size in row_tiles(width, 352):
        tile = dot_nt(wide[at : at + size, :], wide[...])
        if base is not None:
            tile = tile + base[at : at + size, :]
        tile = tile * scale
        gram[at : at + size, :] = tile.astype(jnp.bfloat16)
        row = lax.broadcasted_iota(jnp.int32, tile.shape, 0) + at
        column = lax.broadcasted_iota(jnp.int32, tile.shape, 1)
        trace = trace + jnp.sum(jnp.where(row == column, tile, 0.0))
        squares = squares + jnp.sum(tile * tile)
    return trace, squares


def grad_kernel(scale, rows, high, m, where, q_mine, q_other, w_mine, w_other, left, wide, gram, poly, all_rows):
    width = gram.shape[0]
    half = w_mine.shape[1]
    lay_out([q_mine, q_other], wide)
    trace, squares = factor_gram(wide, None, gram, scale)
    norm, shift = damping_terms(trace, squares, width)
    rounds = half // rows
    at = lax.broadcasted_iota(jnp.int32, (width, width), 0)
    piece = at // rows
    arrival, other = piece % rounds, piece // rounds
    shard = ((arrival % high) ^ where[0]) * m + 2 * (arrival // high) + (other ^ where[1])
    place = shard * rows + at % rows
    hot = (place == lax.broadcasted_iota(jnp.int32, (width, width), 1)).astype(jnp.float32)
    hot = hot.astype(jnp.bfloat16)
    own = hot[:half]
    y1 = norm * dot_nn(own, gram[...]) + shift * own.astype(jnp.float32)
    y1_low = y1.astype(jnp.bfloat16)
    y2 = norm * dot_nn(y1_low, gram[...]) + shift * y1
    y2_low = y2.astype(jnp.bfloat16)
    y3 = norm * dot_nn(y2_low, gram[...]) + shift * y2
    total = (4.0 * y2 - 6.0 * y1 - y3).astype(jnp.bfloat16)
    poly[...] = dot_nt(total, hot).astype(jnp.bfloat16)
    all_rows[:, :half] = w_mine[...]
    all_rows[:, half:] = w_other[...]
    for at, size in row_tiles(left.shape[0], 352):
        mixed = dot_nt(all_rows[at : at + size, :], poly[...])
        mixed = mixed + 4.0 * w_mine[at : at + size, :].astype(jnp.float32)
        left[at : at + size, :] = mixed.astype(jnp.bfloat16)


def act_kernel(scale, parts, base, left, w_mine, *refs):
    *refs, update, inner, wide, gram, first, second = refs
    lay_out(refs, wide)
    width = gram.shape[0]
    trace, squares = factor_gram(wide, base, gram, scale)
    norm, shift = damping_terms(trace, squares, width)
    tiles = row_tiles(width, 352)
    for at, size in tiles:
        rows = left[at : at + size, :].astype(jnp.float32)
        step = norm * dot_nn(gram[at : at + size, :], left[...]) + shift * rows
        first[at : at + size, :] = 4.0 * rows - step
    second[...] = first[...].astype(jnp.bfloat16)
    total = 0.0
    for at, size in tiles:
        rows = left[at : at + size, :].astype(jnp.float32)
        step = norm * dot_nn(gram[at : at + size, :], second[...])
        first[at : at + size, :] = step + shift * first[at : at + size, :] - 6.0 * rows
    second[...] = first[...].astype(jnp.bfloat16)
    for at, size in tiles:
        rows = left[at : at + size, :].astype(jnp.float32)
        step = norm * dot_nn(gram[at : at + size, :], second[...])
        done = step + shift * first[at : at + size, :] + 4.0 * rows
        total = total + jnp.sum(done * w_mine[at : at + size, :].astype(jnp.float32))
        update[at : at + size, :] = done.astype(jnp.bfloat16)
    inner[...] = jnp.full(inner.shape, total, jnp.float32)


def call(kernel, out_shape, scratch, operands, flops, scalars=0):
    vmem = pl.BlockSpec(memory_space=pltpu.VMEM)
    smem = pl.BlockSpec(memory_space=pltpu.SMEM)
    moved = sum(x.size * x.dtype.itemsize for x in operands)
    return pl.pallas_call(
        kernel,
        out_shape=out_shape,
        in_specs=[smem] * scalars + [vmem] * (len(operands) - scalars),
        out_specs=jax.tree.map(lambda _: vmem, out_shape),
        scratch_shapes=[pltpu.VMEM(shape, dtype) for shape, dtype in scratch],
        compiler_params=pltpu.CompilerParams(vmem_limit_bytes=48 * 2**20),
        cost_estimate=pl.CostEstimate(flops=flops, bytes_accessed=moved, transcendentals=0),
    )(*operands)


def per_device(hidden_acts, out_grads, sample_idx, grad_weight, momentum, weight):
    n = lax.axis_size("shard")
    nt = lax.axis_size("tensor")
    batches, picks = sample_idx.shape
    rows, hidden = grad_weight.shape
    blocks = hidden // ABLK
    high = 2 * blocks
    m = n // high
    me = lax.axis_index("shard")
    col = lax.axis_index("tensor")
    core = col % 2
    hi = me // m
    lo = me % m

    def pairs_of(f):
        def target(s, t):
            to = f(s // m, s % m, t // 2, t % 2)
            return None if to is None else (to[0] * m + to[1], to[2] * 2 + to[3])

        return route(n, nt, target)

    def send(value, f, back=False):
        pairs = pairs_of(f)
        if back:
            pairs = [(to, source) for source, to in pairs]
        return lax.ppermute(value, AXES, pairs)

    def over_lo(value, d):
        return send(value, lambda h, l, y, c: (h, l ^ d, y, c))

    def over_core(value):
        return send(value, lambda h, l, y, c: (h, l, y, c ^ 1))

    def home(p):
        def target(h, l, y, c):
            j = h ^ (p % high)
            if l // 2 != p // high or j > 1:
                return None
            return (1 + j, c, y, l % 2)

        return target

    rounds = n // 2
    mine_j = hi - 1
    at_home = jnp.logical_and(jnp.logical_or(hi == 1, hi == 2), lo < 2)

    grad_t = grad_weight.T.reshape(blocks, ABLK, rows)
    w_own = [
        send(lax.dynamic_index_in_dim(grad_t, (hi ^ p) & 1, 0, keepdims=False), home(p))
        for p in range(rounds)
    ]

    acts_t = jnp.swapaxes(hidden_acts, 1, 2)
    tokens_t = lax.dynamic_index_in_dim(out_grads, col // 2, 0, keepdims=False).T
    my_idx = lax.dynamic_index_in_dim(sample_idx, col // 2, 0, keepdims=False)
    q = pick_transposed(tokens_t, my_idx)
    q = [
        send(q, lambda h, l, y, c, p=p: (1 + c, l, y, h & 1) if h >> 1 == p else None)
        for p in range(high // 2)
    ]
    q = jnp.stack(q)

    picked = jnp.stack([pick_transposed(acts_t[i], sample_idx[i]) for i in range(batches)])
    picked = picked.reshape(batches, blocks, ABLK, picks)
    z_own = [
        send(lax.dynamic_index_in_dim(picked, (hi ^ p) & 1, 1, keepdims=False), home(p))
        for p in range(rounds)
    ]

    q = jnp.concatenate([q] + [over_lo(q, d) for d in range(1, m)])
    q = jnp.concatenate(
        [q] + [send(q, lambda h, l, y, c, d=d: (h, l, y ^ d, c)) for d in range(1, nt // 2)]
    )
    q_other = over_core(q)

    w_mine = jnp.concatenate(w_own, axis=1)
    w_other = over_core(w_mine)

    bf16, f32 = jnp.bfloat16, jnp.float32
    count = batches * picks * n
    scale = 1.0 / count
    half = rounds * rows
    where = jnp.stack([mine_j & 1, core]).astype(jnp.int32)
    left = call(
        functools.partial(grad_kernel, scale, rows, high, m),
        jax.ShapeDtypeStruct((ABLK, half), bf16),
        [((DOUT, count), bf16), ((DOUT, DOUT), bf16), ((half, DOUT), bf16), ((ABLK, DOUT), bf16)],
        [where, q, q_other, w_mine, w_other],
        2 * DOUT * (DOUT * count + 4 * half * DOUT + ABLK * half),
        scalars=1,
    )

    cut = rounds // 2
    z_first = z_own[:cut] + [over_core(z) for z in z_own[:cut]]
    z_second = z_own[cut:] + [over_core(z) for z in z_own[cut:]]
    base = call(
        gram_kernel,
        jax.ShapeDtypeStruct((ABLK, ABLK), f32),
        [((ABLK, count // 2), bf16)],
        z_first,
        ABLK * ABLK * count,
    )

    update, inner = call(
        functools.partial(act_kernel, scale, len(z_second)),
        (jax.ShapeDtypeStruct((ABLK, half), bf16), jax.ShapeDtypeStruct((8, 128), f32)),
        [
            ((ABLK, count // 2), bf16),
            ((ABLK, ABLK), bf16),
            ((ABLK, half), f32),
            ((ABLK, half), bf16),
        ],
        [base, left, w_mine] + z_second,
        ABLK * ABLK * (count + 6 * half),
    )

    total = jnp.where(at_home, inner[:1, :1], 0.0)
    back = [
        send(update[:, p * rows : (p + 1) * rows], home(p), back=True) for p in range(rounds)
    ]
    total = total + over_core(total)
    for d in [2**i for i in range(10) if 2**i < nt // 2]:
        total = total + send(total, lambda h, l, y, c, d=d: (h, l, y ^ d, c))
    for d in [2**i for i in range(10) if 2**i < m]:
        total = total + over_lo(total, d)
    for d in [2**i for i in range(10) if 2**i < high]:
        total = total + send(total, lambda h, l, y, c, d=d: (h ^ d, l, y, c))
    ratio = jnp.minimum(1.0, CLIP_LEVEL / jnp.sqrt(total[0, 0] / (DOUT * FF)))

    even = sum(x.astype(jnp.float32) for x in back[0::2])
    odd = sum(x.astype(jnp.float32) for x in back[1::2])
    swap = (hi & 1) == 1
    final = jnp.concatenate([jnp.where(swap, odd, even), jnp.where(swap, even, odd)], axis=0)
    new_momentum = MOMENTUM_RATE * momentum.T + ratio * final
    new_weight = weight.T - LEARN_RATE * new_momentum
    return (new_momentum.T, new_weight.T)


def solution(mesh):
    in_specs = (
        P(None, "shard", "tensor"),
        P(None, "shard", None),
        P(None, "shard"),
        P("shard", "tensor"),
        P("shard", "tensor"),
        P("shard", "tensor"),
    )
    out_specs = (P("shard", "tensor"), P("shard", "tensor"))
    return jax.shard_map(
        per_device, mesh=mesh, in_specs=in_specs, out_specs=out_specs, check_vma=False
    )
```

```python
import functools

import jax
import jax.numpy as jnp
from jax import lax
from jax.experimental import pallas as pl
from jax.experimental.pallas import tpu as pltpu
from jax.sharding import PartitionSpec as P

DOUT = 1024
FF = 10944
ABLK = 1368

DAMPING = 0.1
CLIP_LEVEL = 0.5
MOMENTUM_RATE = 0.9
LEARN_RATE = 0.5

AXES = ("shard", "tensor")
VMEM_MIB = 32
ORDER = (0, 2, 3, 1)


def mirrored(position, j):
    return position + j * (len(ORDER) - 1 - 2 * position)


def route(shards, tensors, target):
    pairs = []
    for s in range(shards):
        for t in range(tensors):
            to = target(s, t)
            if to is not None:
                pairs.append((s * tensors + t, to[0] * tensors + to[1]))
    return pairs


def pick_transposed(tokens_t, where):
    hot = (where[None, :] == lax.broadcasted_iota(jnp.int32, (tokens_t.shape[1], where.shape[0]), 0))
    return jnp.dot(tokens_t, hot.astype(jnp.bfloat16), preferred_element_type=jnp.float32).astype(
        jnp.bfloat16
    )


def row_tiles(width, limit):
    count = -(-width // limit)
    size = -(-width // (count * 16)) * 16
    return [(at, min(size, width - at)) for at in range(0, width, size)]


def dot_nt(a, b):
    return lax.dot_general(a, b, (((1,), (1,)), ((), ())), preferred_element_type=jnp.float32)


def dot_nn(a, b):
    return jnp.dot(a, b, preferred_element_type=jnp.float32)


def damping_terms(trace, squares, width):
    shift = DAMPING * trace / width
    norm = jnp.sqrt(squares + 2.0 * shift * trace + width * shift * shift)
    return 1.0 / norm, shift / norm


def lay_out(parts, wide):
    at = 0
    for part in parts:
        count, _, lanes = part.shape
        for i in range(count):
            wide[:, at : at + lanes] = part[i]
            at += lanes


def gram_kernel(*refs):
    *parts, out, wide = refs
    lay_out(parts, wide)
    for at, size in row_tiles(out.shape[0], 352):
        out[at : at + size, :] = dot_nt(wide[at : at + size, :], wide[...])


def factor_gram(wide, base, gram, scale):
    width = gram.shape[0]
    trace, squares = 0.0, 0.0
    for at, size in row_tiles(width, 352):
        tile = dot_nt(wide[at : at + size, :], wide[...])
        if base is not None:
            tile = tile + base[at : at + size, :]
        tile = tile * scale
        gram[at : at + size, :] = tile.astype(jnp.bfloat16)
        row = lax.broadcasted_iota(jnp.int32, tile.shape, 0) + at
        column = lax.broadcasted_iota(jnp.int32, tile.shape, 1)
        trace = trace + jnp.sum(jnp.where(row == column, tile, 0.0))
        squares = squares + jnp.sum(tile * tile)
    return trace, squares


def pick_kernel(upper, index, tokens, outer, inside):
    batches, _, count = tokens.shape
    picks = index.shape[1]
    for i in range(batches):
        row = lax.broadcasted_iota(jnp.int32, (count, picks), 0)
        hot = (row == index[i : i + 1, :]).astype(jnp.float32).astype(jnp.bfloat16)
        chosen = dot_nn(tokens[i], hot)
        for block in range(2):
            part = chosen[block * ABLK : (block + 1) * ABLK].astype(jnp.bfloat16)

            @pl.when(upper[0] == block)
            def _():
                outer[i] = part

            @pl.when(upper[0] != block)
            def _():
                inside[i] = part


def grad_kernel(scale, rows, high, m, where, *refs):
    *q_parts, w_mine, w_other, left, wide, gram, poly, all_rows = refs
    width = gram.shape[0]
    half = w_mine.shape[1]
    lay_out(q_parts, wide)
    trace, squares = factor_gram(wide, None, gram, scale)
    norm, shift = damping_terms(trace, squares, width)
    rounds = half // rows
    at = lax.broadcasted_iota(jnp.int32, (width, width), 0)
    piece = at // rows
    arrival, other = piece % rounds, piece // rounds
    turn = arrival % high
    position = sum(jnp.where(turn == i, ORDER[i], 0) for i in range(high))
    shard = mirrored(position, where[0]) * m + 2 * (arrival // high) + (other ^ where[1])
    place = shard * rows + at % rows
    hot = (place == lax.broadcasted_iota(jnp.int32, (width, width), 1)).astype(jnp.float32)
    hot = hot.astype(jnp.bfloat16)
    own = hot[:half]
    y1 = norm * dot_nn(own, gram[...]) + shift * own.astype(jnp.float32)
    y1_low = y1.astype(jnp.bfloat16)
    y2 = norm * dot_nn(y1_low, gram[...]) + shift * y1
    y2_low = y2.astype(jnp.bfloat16)
    y3 = norm * dot_nn(y2_low, gram[...]) + shift * y2
    total = (4.0 * y2 - 6.0 * y1 - y3).astype(jnp.bfloat16)
    poly[...] = dot_nt(total, hot).astype(jnp.bfloat16)
    all_rows[:, :half] = w_mine[...]
    all_rows[:, half:] = w_other[...]
    for at, size in row_tiles(left.shape[0], 352):
        mixed = dot_nt(all_rows[at : at + size, :], poly[...])
        mixed = mixed + 4.0 * w_mine[at : at + size, :].astype(jnp.float32)
        left[at : at + size, :] = mixed.astype(jnp.bfloat16)


def act_kernel(scale, parts, base, left, w_mine, *refs):
    *refs, update, inner, wide, gram, first, second = refs
    lay_out(refs, wide)
    width = gram.shape[0]
    trace, squares = factor_gram(wide, base, gram, scale)
    norm, shift = damping_terms(trace, squares, width)
    tiles = row_tiles(width, 352)
    for at, size in tiles:
        rows = left[at : at + size, :].astype(jnp.float32)
        step = norm * dot_nn(gram[at : at + size, :], left[...]) + shift * rows
        first[at : at + size, :] = 4.0 * rows - step
    second[...] = first[...].astype(jnp.bfloat16)
    total = 0.0
    for at, size in tiles:
        rows = left[at : at + size, :].astype(jnp.float32)
        step = norm * dot_nn(gram[at : at + size, :], second[...])
        first[at : at + size, :] = step + shift * first[at : at + size, :] - 6.0 * rows
    second[...] = first[...].astype(jnp.bfloat16)
    for at, size in tiles:
        rows = left[at : at + size, :].astype(jnp.float32)
        step = norm * dot_nn(gram[at : at + size, :], second[...])
        done = step + shift * first[at : at + size, :] + 4.0 * rows
        total = total + jnp.sum(done * w_mine[at : at + size, :].astype(jnp.float32))
        update[at : at + size, :] = done.astype(jnp.bfloat16)
    inner[...] = jnp.full(inner.shape, total, jnp.float32)


def call(kernel, out_shape, scratch, operands, flops, scalars=0):
    vmem = pl.BlockSpec(memory_space=pltpu.VMEM)
    smem = pl.BlockSpec(memory_space=pltpu.SMEM)
    moved = sum(x.size * x.dtype.itemsize for x in operands)
    return pl.pallas_call(
        kernel,
        out_shape=out_shape,
        in_specs=[smem] * scalars + [vmem] * (len(operands) - scalars),
        out_specs=jax.tree.map(lambda _: vmem, out_shape),
        scratch_shapes=[pltpu.VMEM(shape, dtype) for shape, dtype in scratch],
        compiler_params=pltpu.CompilerParams(vmem_limit_bytes=VMEM_MIB * 2**20),
        cost_estimate=pl.CostEstimate(flops=flops, bytes_accessed=moved, transcendentals=0),
    )(*operands)


def per_device(hidden_acts, out_grads, sample_idx, grad_weight, momentum, weight):
    n = lax.axis_size("shard")
    nt = lax.axis_size("tensor")
    batches, picks = sample_idx.shape
    rows, hidden = grad_weight.shape
    blocks = hidden // ABLK
    high = 2 * blocks
    m = n // high
    me = lax.axis_index("shard")
    col = lax.axis_index("tensor")
    core = col % 2
    hi = me // m
    lo = me % m

    def pairs_of(f):
        def target(s, t):
            to = f(s // m, s % m, t // 2, t % 2)
            return None if to is None else (to[0] * m + to[1], to[2] * 2 + to[3])

        return route(n, nt, target)

    def send(value, f, back=False):
        pairs = pairs_of(f)
        if back:
            pairs = [(to, source) for source, to in pairs]
        return lax.ppermute(value, AXES, pairs)

    def over_lo(value, d):
        return send(value, lambda h, l, y, c: (h, l ^ d, y, c))

    def over_core(value):
        return send(value, lambda h, l, y, c: (h, l, y, c ^ 1))

    def home(p):
        def target(h, l, y, c):
            j = 0 if h == ORDER[p % high] else 1
            if l // 2 != p // high or h != mirrored(ORDER[p % high], j):
                return None
            return (1 + j, c, y, l % 2)

        return target

    def outer_round(p):
        return p % high in (0, high - 1)

    upper = hi >= high // 2

    def after(value, others):
        return lax.optimization_barrier((value, others))[0]

    rounds = n // 2
    mine_j = hi - 1
    at_home = jnp.logical_and(jnp.logical_or(hi == 1, hi == 2), lo < 2)

    tokens_t = lax.dynamic_index_in_dim(out_grads, col // 2, 0, keepdims=False).T
    my_idx = lax.dynamic_index_in_dim(sample_idx, col // 2, 0, keepdims=False)
    q = pick_transposed(tokens_t, my_idx)
    q_own = [send(q, home(p)) for p in range(rounds)]
    q_same = jnp.stack(q_own)
    q_parts = [q_same, over_core(q_same)]

    bf16, f32 = jnp.bfloat16, jnp.float32
    outer, inside = call(
        pick_kernel,
        (jax.ShapeDtypeStruct((batches, ABLK, picks), bf16),) * 2,
        [],
        [upper.astype(jnp.int32).reshape(1), sample_idx, jnp.swapaxes(hidden_acts, 1, 2)],
        2 * batches * picks * hidden * hidden_acts.shape[1],
        scalars=1,
    )
    late = [p for p in range(rounds) if p % high == 2]
    early = [p for p in range(rounds) if p % high != 2]
    outer, inside = after((outer, inside), q_own)
    z_early = [send(outer if outer_round(p) else inside, home(p)) for p in early]

    grad_t = after(grad_weight.T, z_early)
    first = jnp.where(upper, ABLK, 0)
    w_outer = lax.dynamic_slice_in_dim(grad_t, first, ABLK, 0)
    w_inside = lax.dynamic_slice_in_dim(grad_t, ABLK - first, ABLK, 0)
    w_own = [send(w_outer if outer_round(p) else w_inside, home(p)) for p in range(rounds)]
    w_mine = jnp.concatenate(w_own, axis=1)
    w_other = over_core(w_mine)

    inside = after(inside, w_own)
    z_late = [send(inside, home(p)) for p in late]

    for d in range(1, nt // 2):
        q_far = send(q_same, lambda h, l, y, c, d=d: (h, l, y ^ d, c))
        q_parts += [q_far, over_core(after(q_far, w_own))]

    count = batches * picks * n
    scale = 1.0 / count
    half = rounds * rows
    where = jnp.stack([mine_j & 1, core]).astype(jnp.int32)
    left = call(
        functools.partial(grad_kernel, scale, rows, high, m),
        jax.ShapeDtypeStruct((ABLK, half), bf16),
        [((DOUT, count), bf16), ((DOUT, DOUT), bf16), ((half, DOUT), bf16), ((ABLK, DOUT), bf16)],
        [where, *q_parts, w_mine, w_other],
        2 * DOUT * (DOUT * count + 4 * half * DOUT + ABLK * half),
        scalars=1,
    )

    z_first = z_early + [over_core(z) for z in z_early]
    z_second = z_late + [over_core(z) for z in z_late]
    base = call(
        gram_kernel,
        jax.ShapeDtypeStruct((ABLK, ABLK), f32),
        [((ABLK, count * len(early) // rounds), bf16)],
        z_first,
        2 * ABLK * ABLK * count * len(early) // rounds,
    )

    update, inner = call(
        functools.partial(act_kernel, scale, len(z_second)),
        (jax.ShapeDtypeStruct((ABLK, half), bf16), jax.ShapeDtypeStruct((8, 128), f32)),
        [
            ((ABLK, count * len(late) // rounds), bf16),
            ((ABLK, ABLK), bf16),
            ((ABLK, half), f32),
            ((ABLK, half), bf16),
        ],
        [base, left, w_mine] + z_second,
        2 * ABLK * ABLK * (count * len(late) // rounds + 3 * half),
    )

    back = [
        send(update[:, p * rows : (p + 1) * rows], home(p), back=True) for p in range(rounds)
    ]
    mine = jnp.where(at_home, inner[:1], 0.0)
    heard = lax.all_to_all(jnp.broadcast_to(mine[None], (n * nt, 1, 128)), AXES, 0, 0)
    total = jnp.sum(heard, axis=0)
    ratio = jnp.minimum(1.0, CLIP_LEVEL / jnp.sqrt(total[0, 0] / (DOUT * FF)))

    got_outer = sum(x.astype(f32) for p, x in enumerate(back) if outer_round(p))
    got_inside = sum(x.astype(f32) for p, x in enumerate(back) if not outer_round(p))
    final = jnp.concatenate(
        [jnp.where(upper, got_inside, got_outer), jnp.where(upper, got_outer, got_inside)], axis=0
    )
    new_momentum = MOMENTUM_RATE * momentum.T + ratio * final
    new_weight = weight.T - LEARN_RATE * new_momentum
    return (new_momentum.T, new_weight.T)


def solution(mesh):
    in_specs = (
        P(None, "shard", "tensor"),
        P(None, "shard", None),
        P(None, "shard"),
        P("shard", "tensor"),
        P("shard", "tensor"),
        P("shard", "tensor"),
    )
    out_specs = (P("shard", "tensor"), P("shard", "tensor"))
    return jax.shard_map(
        per_device, mesh=mesh, in_specs=in_specs, out_specs=out_specs, check_vma=False
    )
```

```python
import functools

import jax
import jax.numpy as jnp
from jax import lax
from jax.experimental import pallas as pl
from jax.experimental.pallas import tpu as pltpu
from jax.sharding import PartitionSpec as P

DOUT = 1024
FF = 10944
ABLK = 1368

DAMPING = 0.1
CLIP_LEVEL = 0.5
MOMENTUM_RATE = 0.9
LEARN_RATE = 0.5

AXES = ("shard", "tensor")
ORDER = (0, 2, 3, 1)


def mirrored(position, j):
    return position + j * (len(ORDER) - 1 - 2 * position)


def route(shards, tensors, target):
    pairs = []
    for s in range(shards):
        for t in range(tensors):
            to = target(s, t)
            if to is not None:
                pairs.append((s * tensors + t, to[0] * tensors + to[1]))
    return pairs


def pick_transposed(tokens_t, where):
    hot = (where[None, :] == lax.broadcasted_iota(jnp.int32, (tokens_t.shape[1], where.shape[0]), 0))
    return jnp.dot(tokens_t, hot.astype(jnp.bfloat16), preferred_element_type=jnp.float32).astype(
        jnp.bfloat16
    )


def row_tiles(width, limit):
    count = -(-width // limit)
    size = -(-width // (count * 16)) * 16
    return [(at, min(size, width - at)) for at in range(0, width, size)]


def dot_nt(a, b):
    return lax.dot_general(a, b, (((1,), (1,)), ((), ())), preferred_element_type=jnp.float32)


def dot_nn(a, b):
    return jnp.dot(a, b, preferred_element_type=jnp.float32)


def damping_terms(trace, squares, width):
    shift = DAMPING * trace / width
    norm = jnp.sqrt(squares + 2.0 * shift * trace + width * shift * shift)
    return 1.0 / norm, shift / norm


def lay_out(parts, wide, chunks=None):
    at = 0
    for part in parts:
        lanes = part.shape[2]
        for i in range(part.shape[0]) if chunks is None else chunks:
            wide[:, at : at + lanes] = part[i]
            at += lanes


def gram_kernel(samples, *refs):
    *parts, gram, taken, wide = refs
    rows = taken.shape[1] // len(parts)
    for i, part in enumerate(parts):
        taken[:, i * rows : (i + 1) * rows] = part[samples]
    lay_out(parts, wide, range(samples))
    for at, size in row_tiles(gram.shape[0], 352):
        gram[at : at + size, :] = dot_nt(wide[at : at + size, :], wide[...])


def factor_gram(wide, base, gram, scale):
    width = gram.shape[0]
    trace, squares = 0.0, 0.0
    for at, size in row_tiles(width, 352):
        tile = dot_nt(wide[at : at + size, :], wide[...])
        if base is not None:
            tile = tile + base[at : at + size, :]
        tile = tile * scale
        gram[at : at + size, :] = tile.astype(jnp.bfloat16)
        near = at // 128 * 128
        square = tile[:, near : at + size]
        row = lax.broadcasted_iota(jnp.int32, square.shape, 0) + (at - near)
        column = lax.broadcasted_iota(jnp.int32, square.shape, 1)
        trace = trace + jnp.sum(jnp.where(row == column, square, 0.0))
        squares = squares + jnp.sum(tile * tile)
    return trace, squares


def pick_kernel(upper, index, tokens, grad_rows, outer, inside):
    batches, _, count = tokens.shape
    picks = index.shape[1]

    def put(block, i, value):
        @pl.when(upper[0] == block)
        def _():
            outer[i] = value

        @pl.when(upper[0] != block)
        def _():
            inside[i] = value

    for i in range(batches):
        row = lax.broadcasted_iota(jnp.int32, (count, picks), 0)
        hot = (row == index[i : i + 1, :]).astype(jnp.float32).astype(jnp.bfloat16)
        chosen = dot_nn(tokens[i], hot)
        for block in range(2):
            put(block, i, chosen[block * ABLK : (block + 1) * ABLK].astype(jnp.bfloat16))
    rows = grad_rows[...].astype(jnp.float32)
    for block in range(2):
        put(block, batches, rows[block * ABLK : (block + 1) * ABLK].astype(jnp.bfloat16))


def grad_kernel(scale, rows, high, m, where, *refs):
    *q_parts, poly, wide, gram = refs
    width = gram.shape[0]
    half = poly.shape[0]
    lay_out(q_parts, wide)
    trace, squares = factor_gram(wide, None, gram, scale)
    norm, shift = damping_terms(trace, squares, width)
    rounds = half // rows
    at = lax.broadcasted_iota(jnp.int32, (width, 128), 0)
    piece = at // rows
    arrival, other = piece % rounds, piece // rounds
    late, pair = arrival // (rounds // 2), arrival % (rounds // 2)
    turn = 2 * late + pair % 2
    position = sum(jnp.where(turn == i, p, 0) for i, p in enumerate(ORDER))
    low = 2 * (pair // 2) + (other ^ where[1])
    shard = mirrored(position, where[0]) * m + low
    place = (shard * rows + at % rows)[:, :1]
    hot = (place == lax.broadcasted_iota(jnp.int32, (width, width), 1)).astype(jnp.float32)
    hot = hot.astype(jnp.bfloat16)
    own = hot[:half]
    y1 = norm * dot_nn(own, gram[...]) + shift * own.astype(jnp.float32)
    y1_low = y1.astype(jnp.bfloat16)
    y2 = norm * dot_nn(y1_low, gram[...]) + shift * y1
    y2_low = y2.astype(jnp.bfloat16)
    y3 = norm * dot_nn(y2_low, gram[...]) + shift * y2
    total = (4.0 * y2 - 6.0 * y1 - y3).astype(jnp.bfloat16)
    poly[...] = dot_nt(total, hot).astype(jnp.bfloat16)


def act_kernel(scale, samples, base, poly, taken, *refs):
    *parts, update, inner, all_rows, left, wide, gram, first, second = refs
    width = gram.shape[0]
    half = update.shape[1]
    on_time = taken.shape[1] // 2
    for i in range(2):
        all_rows[:, i * half : i * half + on_time] = taken[:, i * on_time : (i + 1) * on_time]
        late = parts[i * len(parts) // 2 : (i + 1) * len(parts) // 2]
        rows = (half - on_time) // len(late)
        for k, part in enumerate(late):
            at = i * half + on_time + k * rows
            all_rows[:, at : at + rows] = part[samples][:, :rows]
    tiles = row_tiles(width, 352)
    for at, size in tiles:
        mixed = dot_nt(all_rows[at : at + size, :], poly[...])
        mixed = mixed + 4.0 * all_rows[at : at + size, :half].astype(jnp.float32)
        left[at : at + size, :] = mixed.astype(jnp.bfloat16)
    lay_out(parts, wide, range(samples))
    trace, squares = factor_gram(wide, base, gram, scale)
    norm, shift = damping_terms(trace, squares, width)
    for at, size in tiles:
        rows = left[at : at + size, :].astype(jnp.float32)
        step = norm * dot_nn(gram[at : at + size, :], left[...]) + shift * rows
        first[at : at + size, :] = 4.0 * rows - step
    second[...] = first[...].astype(jnp.bfloat16)
    total = 0.0
    for at, size in tiles:
        rows = left[at : at + size, :].astype(jnp.float32)
        step = norm * dot_nn(gram[at : at + size, :], second[...])
        first[at : at + size, :] = step + shift * first[at : at + size, :] - 6.0 * rows
    second[...] = first[...].astype(jnp.bfloat16)
    for at, size in tiles:
        rows = left[at : at + size, :].astype(jnp.float32)
        step = norm * dot_nn(gram[at : at + size, :], second[...])
        done = step + shift * first[at : at + size, :] + 4.0 * rows
        total = total + jnp.sum(done * all_rows[at : at + size, :half].astype(jnp.float32))
        update[at : at + size, :] = done.astype(jnp.bfloat16)
    inner[...] = jnp.full(inner.shape, total, jnp.float32)


def call(kernel, out_shape, scratch, operands, flops, vmem_mib, scalars=0):
    vmem = pl.BlockSpec(memory_space=pltpu.VMEM)
    smem = pl.BlockSpec(memory_space=pltpu.SMEM)
    moved = sum(x.size * x.dtype.itemsize for x in operands)
    return pl.pallas_call(
        kernel,
        out_shape=out_shape,
        in_specs=[smem] * scalars + [vmem] * (len(operands) - scalars),
        out_specs=jax.tree.map(lambda _: vmem, out_shape),
        scratch_shapes=[pltpu.VMEM(shape, dtype) for shape, dtype in scratch],
        compiler_params=pltpu.CompilerParams(vmem_limit_bytes=vmem_mib * 2**20),
        cost_estimate=pl.CostEstimate(flops=flops, bytes_accessed=moved, transcendentals=0),
    )(*operands)


def per_device(hidden_acts, out_grads, sample_idx, grad_weight, momentum, weight):
    n = lax.axis_size("shard")
    nt = lax.axis_size("tensor")
    batches, picks = sample_idx.shape
    rows, hidden = grad_weight.shape
    blocks = hidden // ABLK
    high = 2 * blocks
    m = n // high
    me = lax.axis_index("shard")
    col = lax.axis_index("tensor")
    core = col % 2
    hi = me // m
    lo = me % m

    def pairs_of(f):
        def target(s, t):
            to = f(s // m, s % m, t // 2, t % 2)
            return None if to is None else (to[0] * m + to[1], to[2] * 2 + to[3])

        return route(n, nt, target)

    def send(value, f, back=False):
        pairs = pairs_of(f)
        if back:
            pairs = [(to, source) for source, to in pairs]
        return lax.ppermute(value, AXES, pairs)

    def over_lo(value, d):
        return send(value, lambda h, l, y, c: (h, l ^ d, y, c))

    def over_core(value):
        return send(value, lambda h, l, y, c: (h, l, y, c ^ 1))

    def home(p):
        def target(h, l, y, c):
            j = 0 if h == ORDER[p % high] else 1
            if l // 2 != p // high or h != mirrored(ORDER[p % high], j):
                return None
            return (1 + j, c, y, l % 2)

        return target

    def outer_round(p):
        return p % high in (0, high - 1)

    upper = hi >= high // 2

    def after(value, others):
        return lax.optimization_barrier((value, others))[0]

    rounds = n // 2
    mine_j = hi - 1
    at_home = jnp.logical_and(jnp.logical_or(hi == 1, hi == 2), lo < 2)

    tokens_t = lax.dynamic_index_in_dim(out_grads, col // 2, 0, keepdims=False).T
    my_idx = lax.dynamic_index_in_dim(sample_idx, col // 2, 0, keepdims=False)
    q = pick_transposed(tokens_t, my_idx)
    q_own = [send(q, home(p)) for p in range(rounds)]
    bf16, f32 = jnp.bfloat16, jnp.float32
    assert rows == picks or n > 8
    grad_t = grad_weight.T
    if rows < picks:
        grad_t = jnp.pad(grad_t, ((0, 0), (0, picks - rows)))
    outer, inside = call(
        pick_kernel,
        (jax.ShapeDtypeStruct((batches + 1, ABLK, picks), bf16),) * 2,
        [],
        [upper.astype(jnp.int32).reshape(1), sample_idx, jnp.swapaxes(hidden_acts, 1, 2), grad_t],
        2 * batches * picks * hidden * hidden_acts.shape[1],
        vmem_mib=12,
        scalars=1,
    )
    late = [p for p in range(rounds) if p % high >= 2]
    early = [p for p in range(rounds) if p % high < 2]
    facing = lambda parts: [x for p, x in enumerate(parts) if p % high < 2]
    q_same = after(jnp.stack(q_own), [outer, inside])
    q_far = [
        send(q_same, lambda h, l, y, c, d=d: (h, l, y ^ d, c)) for d in range(1, nt // 2)
    ]
    turn = lambda p, pair: send(pair[0] if outer_round(p) else pair[1], home(p))
    on_time = [turn(p, (outer, inside)) for p in early]

    pair = after((outer, inside), on_time)
    tardy = [turn(p, pair) for p in late]
    on_time_other = [over_core(x) for x in on_time]
    q_parts = [q_same] + q_far
    q_parts = q_parts + [over_core(x) for x in q_parts]

    count = batches * picks * n
    scale = 1.0 / count
    half = rounds * rows
    where = jnp.stack([mine_j & 1, core]).astype(jnp.int32)
    poly = call(
        functools.partial(grad_kernel, scale, rows, high, m),
        jax.ShapeDtypeStruct((half, DOUT), bf16),
        [((DOUT, count), bf16), ((DOUT, DOUT), bf16)],
        [where, *q_parts],
        2 * DOUT * (DOUT * count + 4 * half * DOUT),
        vmem_mib=28 if n == 8 else 46,
        scalars=1,
    )
    share = len(early) / rounds
    base, taken = call(
        functools.partial(gram_kernel, batches),
        (
            jax.ShapeDtypeStruct((ABLK, ABLK), f32),
            jax.ShapeDtypeStruct((ABLK, 2 * len(early) * picks), bf16),
        ),
        [((ABLK, int(count * share)), bf16)],
        on_time + on_time_other,
        int(2 * ABLK * ABLK * count * share),
        vmem_mib=12 if n == 8 else 40,
    )
    if rows < picks:
        taken = taken.reshape(ABLK, -1, picks)[:, :, :rows].reshape(ABLK, -1)

    tardy = after(tardy, [poly, base] + tardy)
    tardy = tardy + [over_core(x) for x in tardy]
    update, inner = call(
        functools.partial(act_kernel, scale, batches),
        (jax.ShapeDtypeStruct((ABLK, half), bf16), jax.ShapeDtypeStruct((8, 128), f32)),
        [
            ((ABLK, DOUT), bf16),
            ((ABLK, half), bf16),
            ((ABLK, count - int(count * share)), bf16),
            ((ABLK, ABLK), bf16),
            ((ABLK, half), f32),
            ((ABLK, half), bf16),
        ],
        [base, poly, taken] + tardy,
        int(2 * ABLK * (ABLK * (count * (1 - share) + 3 * half) + half * DOUT)),
        vmem_mib=28 if n == 8 else 46,
    )

    back = [
        send(update[:, a * rows : (a + 1) * rows], home(p), back=True)
        for p, a in sorted((p, a) for a, p in enumerate(early + late))
    ]
    mine = jnp.where(at_home, inner[:1], 0.0)
    heard = lax.all_to_all(jnp.broadcast_to(mine[None], (n * nt, 1, 128)), AXES, 0, 0)
    total = jnp.sum(heard, axis=0)
    ratio = jnp.minimum(1.0, CLIP_LEVEL / jnp.sqrt(total[0, 0] / (DOUT * FF)))

    got_outer = sum(x.astype(f32) for p, x in enumerate(back) if outer_round(p))
    got_inside = sum(x.astype(f32) for p, x in enumerate(back) if not outer_round(p))
    final = jnp.concatenate(
        [jnp.where(upper, got_inside, got_outer), jnp.where(upper, got_outer, got_inside)], axis=0
    )
    new_momentum = MOMENTUM_RATE * momentum.T + ratio * final
    new_weight = weight.T - LEARN_RATE * new_momentum
    return (new_momentum.T, new_weight.T)


def solution(mesh):
    in_specs = (
        P(None, "shard", "tensor"),
        P(None, "shard", None),
        P(None, "shard"),
        P("shard", "tensor"),
        P("shard", "tensor"),
        P("shard", "tensor"),
    )
    out_specs = (P("shard", "tensor"), P("shard", "tensor"))
    return jax.shard_map(
        per_device, mesh=mesh, in_specs=in_specs, out_specs=out_specs, check_vma=False
    )
```

```python
import functools

import jax
import jax.numpy as jnp
from jax import lax
from jax.experimental import pallas as pl
from jax.experimental.pallas import tpu as pltpu
from jax.sharding import PartitionSpec as P

DOUT = 1024
FF = 10944
ABLK = 1368

DAMPING = 0.1
CLIP_LEVEL = 0.5
MOMENTUM_RATE = 0.9
LEARN_RATE = 0.5

AXES = ("shard", "tensor")
ORDER = (0, 2, 3, 1)


def mirrored(position, j):
    return position + j * (len(ORDER) - 1 - 2 * position)


def route(shards, tensors, target):
    pairs = []
    for s in range(shards):
        for t in range(tensors):
            to = target(s, t)
            if to is not None:
                pairs.append((s * tensors + t, to[0] * tensors + to[1]))
    return pairs


def pick_transposed(tokens_t, where):
    hot = (where[None, :] == lax.broadcasted_iota(jnp.int32, (tokens_t.shape[1], where.shape[0]), 0))
    return jnp.dot(tokens_t, hot.astype(jnp.bfloat16), preferred_element_type=jnp.float32).astype(
        jnp.bfloat16
    )


def row_tiles(width, limit):
    count = -(-width // limit)
    size = -(-width // (count * 16)) * 16
    return [(at, min(size, width - at)) for at in range(0, width, size)]


def dot_nt(a, b):
    return lax.dot_general(a, b, (((1,), (1,)), ((), ())), preferred_element_type=jnp.float32)


def dot_nn(a, b):
    return jnp.dot(a, b, preferred_element_type=jnp.float32)


def damping_terms(trace, squares, width):
    shift = DAMPING * trace / width
    norm = jnp.sqrt(squares + 2.0 * shift * trace + width * shift * shift)
    return 1.0 / norm, shift / norm


def lay_out(parts, wide, chunks=None):
    at = 0
    for part in parts:
        lanes = part.shape[2]
        for i in range(part.shape[0]) if chunks is None else chunks:
            wide[:, at : at + lanes] = part[i]
            at += lanes


def gram_kernel(samples, *refs):
    *parts, gram, taken, wide = refs
    rows = taken.shape[1] // len(parts)
    for i, part in enumerate(parts):
        taken[:, i * rows : (i + 1) * rows] = part[samples]
    lay_out(parts, wide, range(samples))
    for at, size in row_tiles(gram.shape[0], 352):
        gram[at : at + size, :] = dot_nt(wide[at : at + size, :], wide[...])


def factor_gram(wide, base, gram, scale):
    width = gram.shape[0]
    trace, squares = 0.0, 0.0
    for at, size in row_tiles(width, 352):
        tile = dot_nt(wide[at : at + size, :], wide[...])
        if base is not None:
            tile = tile + base[at : at + size, :]
        tile = tile * scale
        gram[at : at + size, :] = tile.astype(jnp.bfloat16)
        near = at // 128 * 128
        square = tile[:, near : at + size]
        row = lax.broadcasted_iota(jnp.int32, square.shape, 0) + (at - near)
        column = lax.broadcasted_iota(jnp.int32, square.shape, 1)
        trace = trace + jnp.sum(jnp.where(row == column, square, 0.0))
        squares = squares + jnp.sum(tile * tile)
    return trace, squares


def pick_kernel(upper, index, tokens, grad_rows, outer, inside):
    batches, _, count = tokens.shape
    picks = index.shape[1]

    def put(block, i, value):
        @pl.when(upper[0] == block)
        def _():
            outer[i] = value

        @pl.when(upper[0] != block)
        def _():
            inside[i] = value

    for i in range(batches):
        row = lax.broadcasted_iota(jnp.int32, (count, picks), 0)
        hot = (row == index[i : i + 1, :]).astype(jnp.float32).astype(jnp.bfloat16)
        chosen = dot_nn(tokens[i], hot)
        for block in range(2):
            put(block, i, chosen[block * ABLK : (block + 1) * ABLK].astype(jnp.bfloat16))
    rows = grad_rows[...].astype(jnp.float32)
    for block in range(2):
        put(block, batches, rows[block * ABLK : (block + 1) * ABLK].astype(jnp.bfloat16))


def grad_kernel(scale, rows, high, m, where, *refs):
    *q_parts, poly, wide, gram = refs
    width = gram.shape[0]
    half = poly.shape[0]
    lay_out(q_parts, wide)
    trace, squares = factor_gram(wide, None, gram, scale)
    norm, shift = damping_terms(trace, squares, width)
    rounds = half // rows
    at = lax.broadcasted_iota(jnp.int32, (width, 128), 0)
    piece = at // rows
    arrival, other = piece % rounds, piece // rounds
    late, pair = arrival // (rounds // 2), arrival % (rounds // 2)
    turn = 2 * late + pair % 2
    position = sum(jnp.where(turn == i, p, 0) for i, p in enumerate(ORDER))
    low = 2 * (pair // 2) + (other ^ where[1])
    shard = mirrored(position, where[0]) * m + low
    place = (shard * rows + at % rows)[:, :1]
    hot = (place == lax.broadcasted_iota(jnp.int32, (width, width), 1)).astype(jnp.float32)
    hot = hot.astype(jnp.bfloat16)
    own = hot[:half]
    y1 = norm * dot_nn(own, gram[...]) + shift * own.astype(jnp.float32)
    y1_low = y1.astype(jnp.bfloat16)
    y2 = norm * dot_nn(y1_low, gram[...]) + shift * y1
    y2_low = y2.astype(jnp.bfloat16)
    y3 = norm * dot_nn(y2_low, gram[...]) + shift * y2
    total = (4.0 * y2 - 6.0 * y1 - y3).astype(jnp.bfloat16)
    poly[...] = dot_nt(total, hot).astype(jnp.bfloat16)


def act_kernel(scale, samples, update_rows, base, poly, taken, *refs):
    *refs, inner, all_rows, left, wide, gram, first, second = refs
    width, half = left.shape
    outs = half // update_rows
    parts, update = refs[:-outs], refs[-outs:]
    on_time = taken.shape[1] // 2
    for i in range(2):
        all_rows[:, i * half : i * half + on_time] = taken[:, i * on_time : (i + 1) * on_time]
        late = parts[i * len(parts) // 2 : (i + 1) * len(parts) // 2]
        rows = (half - on_time) // len(late)
        for k, part in enumerate(late):
            at = i * half + on_time + k * rows
            all_rows[:, at : at + rows] = part[samples][:, :rows]
    tiles = row_tiles(width, 352)
    for at, size in tiles:
        mixed = dot_nt(all_rows[at : at + size, :], poly[...])
        mixed = mixed + 4.0 * all_rows[at : at + size, :half].astype(jnp.float32)
        left[at : at + size, :] = mixed.astype(jnp.bfloat16)
    lay_out(parts, wide, range(samples))
    trace, squares = factor_gram(wide, base, gram, scale)
    norm, shift = damping_terms(trace, squares, width)
    for at, size in tiles:
        rows = left[at : at + size, :].astype(jnp.float32)
        step = norm * dot_nn(gram[at : at + size, :], left[...]) + shift * rows
        first[at : at + size, :] = 4.0 * rows - step
    second[...] = first[...].astype(jnp.bfloat16)
    total = 0.0
    for at, size in tiles:
        rows = left[at : at + size, :].astype(jnp.float32)
        step = norm * dot_nn(gram[at : at + size, :], second[...])
        first[at : at + size, :] = step + shift * first[at : at + size, :] - 6.0 * rows
    second[...] = first[...].astype(jnp.bfloat16)
    for at, size in tiles:
        rows = left[at : at + size, :].astype(jnp.float32)
        step = norm * dot_nn(gram[at : at + size, :], second[...])
        done = step + shift * first[at : at + size, :] + 4.0 * rows
        total = total + jnp.sum(done * all_rows[at : at + size, :half].astype(jnp.float32))
        for k, out in enumerate(update):
            out[at : at + size, :] = done[:, k * update_rows : (k + 1) * update_rows].astype(jnp.bfloat16)
    inner[...] = jnp.full(inner.shape, total, jnp.float32)


def call(kernel, out_shape, scratch, operands, flops, vmem_mib, scalars=0):
    vmem = pl.BlockSpec(memory_space=pltpu.VMEM)
    smem = pl.BlockSpec(memory_space=pltpu.SMEM)
    moved = sum(x.size * x.dtype.itemsize for x in operands)
    return pl.pallas_call(
        kernel,
        out_shape=out_shape,
        in_specs=[smem] * scalars + [vmem] * (len(operands) - scalars),
        out_specs=jax.tree.map(lambda _: vmem, out_shape),
        scratch_shapes=[pltpu.VMEM(shape, dtype) for shape, dtype in scratch],
        compiler_params=pltpu.CompilerParams(vmem_limit_bytes=vmem_mib * 2**20),
        cost_estimate=pl.CostEstimate(flops=flops, bytes_accessed=moved, transcendentals=0),
    )(*operands)


def per_device(hidden_acts, out_grads, sample_idx, grad_weight, momentum, weight):
    n = lax.axis_size("shard")
    nt = lax.axis_size("tensor")
    batches, picks = sample_idx.shape
    rows, hidden = grad_weight.shape
    blocks = hidden // ABLK
    high = 2 * blocks
    m = n // high
    me = lax.axis_index("shard")
    col = lax.axis_index("tensor")
    core = col % 2
    hi = me // m
    lo = me % m

    def pairs_of(f):
        def target(s, t):
            to = f(s // m, s % m, t // 2, t % 2)
            return None if to is None else (to[0] * m + to[1], to[2] * 2 + to[3])

        return route(n, nt, target)

    def send(value, f, back=False):
        pairs = pairs_of(f)
        if back:
            pairs = [(to, source) for source, to in pairs]
        return lax.ppermute(value, AXES, pairs)

    def over_lo(value, d):
        return send(value, lambda h, l, y, c: (h, l ^ d, y, c))

    def over_core(value):
        return send(value, lambda h, l, y, c: (h, l, y, c ^ 1))

    def home(p):
        def target(h, l, y, c):
            j = 0 if h == ORDER[p % high] else 1
            if l // 2 != p // high or h != mirrored(ORDER[p % high], j):
                return None
            return (1 + j, c, y, l % 2)

        return target

    def outer_round(p):
        return p % high in (0, high - 1)

    upper = hi >= high // 2

    def after(value, others):
        return lax.optimization_barrier((value, others))[0]

    rounds = n // 2
    mine_j = hi - 1
    at_home = jnp.logical_and(jnp.logical_or(hi == 1, hi == 2), lo < 2)

    tokens_t = lax.dynamic_index_in_dim(out_grads, col // 2, 0, keepdims=False).T
    my_idx = lax.dynamic_index_in_dim(sample_idx, col // 2, 0, keepdims=False)
    q = pick_transposed(tokens_t, my_idx)
    q_own = [send(q, home(p)) for p in range(rounds)]
    bf16, f32 = jnp.bfloat16, jnp.float32
    assert rows == picks or n > 8
    grad_t = grad_weight.T
    if rows < picks:
        grad_t = jnp.pad(grad_t, ((0, 0), (0, picks - rows)))
    outer, inside = call(
        pick_kernel,
        (jax.ShapeDtypeStruct((batches + 1, ABLK, picks), bf16),) * 2,
        [],
        [upper.astype(jnp.int32).reshape(1), sample_idx, jnp.swapaxes(hidden_acts, 1, 2), grad_t],
        2 * batches * picks * hidden * hidden_acts.shape[1],
        vmem_mib=12,
        scalars=1,
    )
    late = [p for p in range(rounds) if p % high >= 2]
    early = [p for p in range(rounds) if p % high < 2]
    facing = lambda parts: [x for p, x in enumerate(parts) if p % high < 2]
    q_same = after(jnp.stack(q_own), [outer, inside])
    q_far = [
        send(q_same, lambda h, l, y, c, d=d: (h, l, y ^ d, c)) for d in range(1, nt // 2)
    ]
    turn = lambda p, pair: send(pair[0] if outer_round(p) else pair[1], home(p))
    on_time = [turn(p, (outer, inside)) for p in early]

    pair = after((outer, inside), [q_same])
    tardy = [turn(p, pair) for p in late]
    on_time_other = [over_core(x) for x in on_time]
    q_parts = [q_same] + q_far
    q_parts = q_parts + [over_core(x) for x in q_parts]

    count = batches * picks * n
    scale = 1.0 / count
    half = rounds * rows
    where = jnp.stack([mine_j & 1, core]).astype(jnp.int32)
    poly = call(
        functools.partial(grad_kernel, scale, rows, high, m),
        jax.ShapeDtypeStruct((half, DOUT), bf16),
        [((DOUT, count), bf16), ((DOUT, DOUT), bf16)],
        [where, *q_parts],
        2 * DOUT * (DOUT * count + 4 * half * DOUT),
        vmem_mib=28 if n == 8 else 46,
        scalars=1,
    )
    share = len(early) / rounds
    base, taken = call(
        functools.partial(gram_kernel, batches),
        (
            jax.ShapeDtypeStruct((ABLK, ABLK), f32),
            jax.ShapeDtypeStruct((ABLK, 2 * len(early) * picks), bf16),
        ),
        [((ABLK, int(count * share)), bf16)],
        on_time + on_time_other,
        int(2 * ABLK * ABLK * count * share),
        vmem_mib=12 if n == 8 else 40,
    )
    if rows < picks:
        taken = taken.reshape(ABLK, -1, picks)[:, :, :rows].reshape(ABLK, -1)

    tardy = after(tardy, [poly, base] + tardy)
    tardy = tardy + [over_core(x) for x in tardy]
    piece = rows if rows % 128 == 0 else half
    *update, inner = call(
        functools.partial(act_kernel, scale, batches, piece),
        (jax.ShapeDtypeStruct((ABLK, piece), bf16),) * (half // piece)
        + (jax.ShapeDtypeStruct((8, 128), f32),),
        [
            ((ABLK, DOUT), bf16),
            ((ABLK, half), bf16),
            ((ABLK, count - int(count * share)), bf16),
            ((ABLK, ABLK), bf16),
            ((ABLK, half), f32),
            ((ABLK, half), bf16),
        ],
        [base, poly, taken] + tardy,
        int(2 * ABLK * (ABLK * (count * (1 - share) + 3 * half) + half * DOUT)),
        vmem_mib=28 if n == 8 else 46,
    )

    back = [
        send(update[a * rows // piece][:, a * rows % piece :][:, :rows], home(p), back=True)
        for p, a in sorted((p, a) for a, p in enumerate(early + late))
    ]
    mine = jnp.where(at_home, inner[:1], 0.0)
    heard = lax.all_to_all(jnp.broadcast_to(mine[None], (n * nt, 1, 128)), AXES, 0, 0)
    total = jnp.sum(heard, axis=0)
    ratio = jnp.minimum(1.0, CLIP_LEVEL / jnp.sqrt(total[0, 0] / (DOUT * FF)))

    got_outer = sum(x.astype(f32) for p, x in enumerate(back) if outer_round(p))
    got_inside = sum(x.astype(f32) for p, x in enumerate(back) if not outer_round(p))
    final = jnp.concatenate(
        [jnp.where(upper, got_inside, got_outer), jnp.where(upper, got_outer, got_inside)], axis=0
    )
    new_momentum = MOMENTUM_RATE * momentum.T + ratio * final
    new_weight = weight.T - LEARN_RATE * new_momentum
    return (new_momentum.T, new_weight.T)


def solution(mesh):
    in_specs = (
        P(None, "shard", "tensor"),
        P(None, "shard", None),
        P(None, "shard"),
        P("shard", "tensor"),
        P("shard", "tensor"),
        P("shard", "tensor"),
    )
    out_specs = (P("shard", "tensor"), P("shard", "tensor"))
    return jax.shard_map(
        per_device, mesh=mesh, in_specs=in_specs, out_specs=out_specs, check_vma=False
    )
```

```python
import functools

import jax
import jax.numpy as jnp
from jax import lax
from jax.experimental import pallas as pl
from jax.experimental.pallas import tpu as pltpu
from jax.sharding import PartitionSpec as P

DOUT = 1024
FF = 10944
ABLK = 1368

DAMPING = 0.1
CLIP_LEVEL = 0.5
MOMENTUM_RATE = 0.9
LEARN_RATE = 0.5

AXES = ("shard", "tensor")
ORDER = (0, 2, 3, 1)


def mirrored(position, j):
    return position + j * (len(ORDER) - 1 - 2 * position)


def route(shards, tensors, target):
    pairs = []
    for s in range(shards):
        for t in range(tensors):
            to = target(s, t)
            if to is not None:
                pairs.append((s * tensors + t, to[0] * tensors + to[1]))
    return pairs


def pick_transposed(tokens_t, where):
    hot = (where[None, :] == lax.broadcasted_iota(jnp.int32, (tokens_t.shape[1], where.shape[0]), 0))
    return jnp.dot(tokens_t, hot.astype(jnp.bfloat16), preferred_element_type=jnp.float32).astype(
        jnp.bfloat16
    )


def row_tiles(width, limit):
    count = -(-width // limit)
    size = -(-width // (count * 16)) * 16
    return [(at, min(size, width - at)) for at in range(0, width, size)]


def dot_nt(a, b):
    return lax.dot_general(a, b, (((1,), (1,)), ((), ())), preferred_element_type=jnp.float32)


def dot_nn(a, b):
    return jnp.dot(a, b, preferred_element_type=jnp.float32)


def damping_terms(trace, squares, width):
    shift = DAMPING * trace / width
    norm = jnp.sqrt(squares + 2.0 * shift * trace + width * shift * shift)
    return 1.0 / norm, shift / norm


def lay_out(parts, wide, chunks=None):
    at = 0
    for part in parts:
        lanes = part.shape[2]
        for i in range(part.shape[0]) if chunks is None else chunks:
            wide[:, at : at + lanes] = part[i]
            at += lanes


def gram_kernel(samples, *refs):
    *parts, gram, taken, wide = refs
    rows = taken.shape[1] // len(parts)
    for i, part in enumerate(parts):
        taken[:, i * rows : (i + 1) * rows] = part[samples]
    lay_out(parts, wide, range(samples))
    for at, size in row_tiles(gram.shape[0], 352):
        gram[at : at + size, :] = dot_nt(wide[at : at + size, :], wide[...])


def more_gram_kernel(samples, base, *refs):
    *parts, gram, wide = refs
    lay_out(parts, wide, range(samples))
    for at, size in row_tiles(gram.shape[0], 352):
        gram[at : at + size, :] = base[at : at + size, :] + dot_nt(wide[at : at + size, :], wide[...])


def factor_gram(wide, base, gram, scale):
    width = gram.shape[0]
    trace, squares = 0.0, 0.0
    for at, size in row_tiles(width, 352):
        tile = dot_nt(wide[at : at + size, :], wide[...])
        if base is not None:
            tile = tile + base[at : at + size, :]
        tile = tile * scale
        gram[at : at + size, :] = tile.astype(jnp.bfloat16)
        near = at // 128 * 128
        square = tile[:, near : at + size]
        row = lax.broadcasted_iota(jnp.int32, square.shape, 0) + (at - near)
        column = lax.broadcasted_iota(jnp.int32, square.shape, 1)
        trace = trace + jnp.sum(jnp.where(row == column, square, 0.0))
        squares = squares + jnp.sum(tile * tile)
    return trace, squares


def pick_kernel(upper, index, tokens, grad_rows, outer, inside):
    batches, _, count = tokens.shape
    picks = index.shape[1]

    def put(block, i, value):
        @pl.when(upper[0] == block)
        def _():
            outer[i] = value

        @pl.when(upper[0] != block)
        def _():
            inside[i] = value

    for i in range(batches):
        row = lax.broadcasted_iota(jnp.int32, (count, picks), 0)
        hot = (row == index[i : i + 1, :]).astype(jnp.float32).astype(jnp.bfloat16)
        chosen = dot_nn(tokens[i], hot)
        for block in range(2):
            put(block, i, chosen[block * ABLK : (block + 1) * ABLK].astype(jnp.bfloat16))
    rows = grad_rows[...].astype(jnp.float32)
    for block in range(2):
        put(block, batches, rows[block * ABLK : (block + 1) * ABLK].astype(jnp.bfloat16))


def grad_kernel(scale, rows, high, m, where, *refs):
    *q_parts, taken, poly, left, wide, gram = refs
    width = gram.shape[0]
    half = poly.shape[0]
    lay_out(q_parts, wide)
    trace, squares = factor_gram(wide, None, gram, scale)
    norm, shift = damping_terms(trace, squares, width)
    rounds = half // rows
    at = lax.broadcasted_iota(jnp.int32, (width, 128), 0)
    piece = at // rows
    arrival, other = piece % rounds, piece // rounds
    late, pair = arrival // (rounds // 2), arrival % (rounds // 2)
    turn = 2 * late + pair % 2
    position = sum(jnp.where(turn == i, p, 0) for i, p in enumerate(ORDER))
    low = 2 * (pair // 2) + (other ^ where[1])
    shard = mirrored(position, where[0]) * m + low
    place = (shard * rows + at % rows)[:, :1]
    hot = (place == lax.broadcasted_iota(jnp.int32, (width, width), 1)).astype(jnp.float32)
    hot = hot.astype(jnp.bfloat16)
    own = hot[:half]
    y1 = norm * dot_nn(own, gram[...]) + shift * own.astype(jnp.float32)
    y1_low = y1.astype(jnp.bfloat16)
    y2 = norm * dot_nn(y1_low, gram[...]) + shift * y1
    y2_low = y2.astype(jnp.bfloat16)
    y3 = norm * dot_nn(y2_low, gram[...]) + shift * y2
    total = (4.0 * y2 - 6.0 * y1 - y3).astype(jnp.bfloat16)
    poly[...] = dot_nt(total, hot).astype(jnp.bfloat16)
    on_time = taken.shape[1] // 2
    for at, size in row_tiles(left.shape[0], 352):
        own = taken[at : at + size, :on_time]
        mixed = dot_nt(own, poly[:, :on_time])
        mixed = mixed + dot_nt(taken[at : at + size, on_time:], poly[:, half : half + on_time])
        left[at : at + size, :on_time] = mixed[:, :on_time] + 4.0 * own.astype(jnp.float32)
        left[at : at + size, on_time:] = mixed[:, on_time:]


def act_kernel(scale, samples, update_rows, base, poly, early, taken, *refs):
    *refs, inner, all_rows, left, wide, gram, first, second = refs
    width, half = left.shape
    outs = half // update_rows
    parts, update = refs[:-outs], refs[-outs:]
    on_time = taken.shape[1] // 2
    for i in range(2):
        all_rows[:, i * half : i * half + on_time] = taken[:, i * on_time : (i + 1) * on_time]
        late = parts[i * len(parts) // 2 : (i + 1) * len(parts) // 2]
        rows = (half - on_time) // len(late)
        for k, part in enumerate(late):
            at = i * half + on_time + k * rows
            all_rows[:, at : at + rows] = part[samples][:, :rows]
    tiles = row_tiles(width, 352)
    for at, size in tiles:
        own = all_rows[at : at + size, on_time:half]
        mixed = early[at : at + size, :] + dot_nt(own, poly[:, on_time:half])
        mixed = mixed + dot_nt(all_rows[at : at + size, half + on_time :], poly[:, half + on_time :])
        left[at : at + size, :on_time] = mixed[:, :on_time].astype(jnp.bfloat16)
        mixed = mixed[:, on_time:] + 4.0 * own.astype(jnp.float32)
        left[at : at + size, on_time:] = mixed.astype(jnp.bfloat16)
    lay_out(parts[::2], wide, range(samples))
    trace, squares = factor_gram(wide, base, gram, scale)
    norm, shift = damping_terms(trace, squares, width)
    for at, size in tiles:
        rows = left[at : at + size, :].astype(jnp.float32)
        step = norm * dot_nn(gram[at : at + size, :], left[...]) + shift * rows
        first[at : at + size, :] = 4.0 * rows - step
    second[...] = first[...].astype(jnp.bfloat16)
    total = 0.0
    for at, size in tiles:
        rows = left[at : at + size, :].astype(jnp.float32)
        step = norm * dot_nn(gram[at : at + size, :], second[...])
        first[at : at + size, :] = step + shift * first[at : at + size, :] - 6.0 * rows
    second[...] = first[...].astype(jnp.bfloat16)
    for at, size in tiles:
        rows = left[at : at + size, :].astype(jnp.float32)
        step = norm * dot_nn(gram[at : at + size, :], second[...])
        done = step + shift * first[at : at + size, :] + 4.0 * rows
        total = total + jnp.sum(done * all_rows[at : at + size, :half].astype(jnp.float32))
        for k, out in enumerate(update):
            out[at : at + size, :] = done[:, k * update_rows : (k + 1) * update_rows].astype(jnp.bfloat16)
    inner[...] = jnp.full(inner.shape, total, jnp.float32)


def call(kernel, out_shape, scratch, operands, flops, vmem_mib, scalars=0):
    vmem = pl.BlockSpec(memory_space=pltpu.VMEM)
    smem = pl.BlockSpec(memory_space=pltpu.SMEM)
    moved = sum(x.size * x.dtype.itemsize for x in operands)
    return pl.pallas_call(
        kernel,
        out_shape=out_shape,
        in_specs=[smem] * scalars + [vmem] * (len(operands) - scalars),
        out_specs=jax.tree.map(lambda _: vmem, out_shape),
        scratch_shapes=[pltpu.VMEM(shape, dtype) for shape, dtype in scratch],
        compiler_params=pltpu.CompilerParams(vmem_limit_bytes=vmem_mib * 2**20),
        cost_estimate=pl.CostEstimate(flops=flops, bytes_accessed=moved, transcendentals=0),
    )(*operands)


def per_device(hidden_acts, out_grads, sample_idx, grad_weight, momentum, weight):
    n = lax.axis_size("shard")
    nt = lax.axis_size("tensor")
    batches, picks = sample_idx.shape
    rows, hidden = grad_weight.shape
    blocks = hidden // ABLK
    high = 2 * blocks
    m = n // high
    me = lax.axis_index("shard")
    col = lax.axis_index("tensor")
    core = col % 2
    hi = me // m
    lo = me % m

    def pairs_of(f):
        def target(s, t):
            to = f(s // m, s % m, t // 2, t % 2)
            return None if to is None else (to[0] * m + to[1], to[2] * 2 + to[3])

        return route(n, nt, target)

    def send(value, f, back=False):
        pairs = pairs_of(f)
        if back:
            pairs = [(to, source) for source, to in pairs]
        return lax.ppermute(value, AXES, pairs)

    def over_lo(value, d):
        return send(value, lambda h, l, y, c: (h, l ^ d, y, c))

    def over_core(value):
        return send(value, lambda h, l, y, c: (h, l, y, c ^ 1))

    def home(p):
        def target(h, l, y, c):
            j = 0 if h == ORDER[p % high] else 1
            if l // 2 != p // high or h != mirrored(ORDER[p % high], j):
                return None
            return (1 + j, c, y, l % 2)

        return target

    def outer_round(p):
        return p % high in (0, high - 1)

    upper = hi >= high // 2

    def after(value, others):
        return lax.optimization_barrier((value, others))[0]

    rounds = n // 2
    mine_j = hi - 1
    at_home = jnp.logical_and(jnp.logical_or(hi == 1, hi == 2), lo < 2)

    tokens_t = lax.dynamic_index_in_dim(out_grads, col // 2, 0, keepdims=False).T
    my_idx = lax.dynamic_index_in_dim(sample_idx, col // 2, 0, keepdims=False)
    q = pick_transposed(tokens_t, my_idx)
    q_own = [send(q, home(p)) for p in range(rounds)]
    bf16, f32 = jnp.bfloat16, jnp.float32
    assert rows == picks or n > 8
    grad_t = grad_weight.T
    if rows < picks:
        grad_t = jnp.pad(grad_t, ((0, 0), (0, picks - rows)))
    outer, inside = call(
        pick_kernel,
        (jax.ShapeDtypeStruct((batches + 1, ABLK, picks), bf16),) * 2,
        [],
        [upper.astype(jnp.int32).reshape(1), sample_idx, jnp.swapaxes(hidden_acts, 1, 2), grad_t],
        2 * batches * picks * hidden * hidden_acts.shape[1],
        vmem_mib=12,
        scalars=1,
    )
    late = [p for p in range(rounds) if p % high >= 2]
    early = [p for p in range(rounds) if p % high < 2]
    facing = lambda parts: [x for p, x in enumerate(parts) if p % high < 2]
    q_same = after(jnp.stack(q_own), [outer, inside])
    q_far = [
        send(q_same, lambda h, l, y, c, d=d: (h, l, y ^ d, c)) for d in range(1, nt // 2)
    ]
    turn = lambda p, pair: send(pair[0] if outer_round(p) else pair[1], home(p))
    on_time = [turn(p, (outer, inside)) for p in early]

    pair = after((outer, inside), [q_same])
    tardy = [turn(p, pair) for p in late]
    on_time_other = [over_core(x) for x in on_time]
    q_parts = [q_same] + q_far
    q_parts = q_parts + [over_core(x) for x in q_parts]

    count = batches * picks * n
    scale = 1.0 / count
    half = rounds * rows
    where = jnp.stack([mine_j & 1, core]).astype(jnp.int32)
    share = len(early) / rounds
    base, taken = call(
        functools.partial(gram_kernel, batches),
        (
            jax.ShapeDtypeStruct((ABLK, ABLK), f32),
            jax.ShapeDtypeStruct((ABLK, 2 * len(early) * picks), bf16),
        ),
        [((ABLK, int(count * share)), bf16)],
        on_time + on_time_other,
        int(2 * ABLK * ABLK * count * share),
        vmem_mib=12 if n == 8 else 40,
    )
    if rows < picks:
        taken = taken.reshape(ABLK, -1, picks)[:, :, :rows].reshape(ABLK, -1)
    poly, left_early = call(
        functools.partial(grad_kernel, scale, rows, high, m),
        (jax.ShapeDtypeStruct((half, DOUT), bf16), jax.ShapeDtypeStruct((ABLK, half), f32)),
        [((DOUT, count), bf16), ((DOUT, DOUT), bf16)],
        [where, *q_parts, taken],
        2 * DOUT * (DOUT * count + 4 * half * DOUT + ABLK * half // 2),
        vmem_mib=28 if n == 8 else 58,
        scalars=1,
    )

    local = [after(x, poly) for x, p in zip(tardy, late) if p % high == 3]
    local = [(x, over_core(x)) for x in local]
    last = [x for x, p in zip(tardy, late) if p % high == 2]
    last = after(last, [poly, base] + last)
    base = after(base, last)
    last = [(x, over_core(x)) for x in last]
    base = call(
        functools.partial(more_gram_kernel, batches),
        jax.ShapeDtypeStruct((ABLK, ABLK), f32),
        [((ABLK, count // 4), bf16)],
        [base] + [x for x, _ in local] + [x for _, x in local],
        2 * ABLK * ABLK * count // 4,
        vmem_mib=12 if n == 8 else 30,
    )
    tardy = [pair[i] for i in range(2) for both in zip(last, local) for pair in both]
    piece = rows if rows % 128 == 0 else half
    *update, inner = call(
        functools.partial(act_kernel, scale, batches, piece),
        (jax.ShapeDtypeStruct((ABLK, piece), bf16),) * (half // piece)
        + (jax.ShapeDtypeStruct((8, 128), f32),),
        [
            ((ABLK, DOUT), bf16),
            ((ABLK, half), bf16),
            ((ABLK, count // 4), bf16),
            ((ABLK, ABLK), bf16),
            ((ABLK, half), f32),
            ((ABLK, half), bf16),
        ],
        [base, poly, left_early, taken] + tardy,
        int(2 * ABLK * (ABLK * (count // 4 + 3 * half) + half * DOUT // 2)),
        vmem_mib=28 if n == 8 else 46,
    )

    back = [
        send(update[a * rows // piece][:, a * rows % piece :][:, :rows], home(p), back=True)
        for p, a in sorted((p, a) for a, p in enumerate(early + late))
    ]
    mine = jnp.where(at_home, inner[:1], 0.0)
    heard = lax.all_to_all(jnp.broadcast_to(mine[None], (n * nt, 1, 128)), AXES, 0, 0)
    total = jnp.sum(heard, axis=0)
    ratio = jnp.minimum(1.0, CLIP_LEVEL / jnp.sqrt(total[0, 0] / (DOUT * FF)))

    got_outer = sum(x.astype(f32) for p, x in reversed(list(enumerate(back))) if outer_round(p))
    got_inside = sum(x.astype(f32) for p, x in reversed(list(enumerate(back))) if not outer_round(p))
    final = jnp.concatenate(
        [jnp.where(upper, got_inside, got_outer), jnp.where(upper, got_outer, got_inside)], axis=0
    )
    new_momentum = MOMENTUM_RATE * momentum.T + ratio * final
    new_weight = weight.T - LEARN_RATE * new_momentum
    return (new_momentum.T, new_weight.T)


def solution(mesh):
    in_specs = (
        P(None, "shard", "tensor"),
        P(None, "shard", None),
        P(None, "shard"),
        P("shard", "tensor"),
        P("shard", "tensor"),
        P("shard", "tensor"),
    )
    out_specs = (P("shard", "tensor"), P("shard", "tensor"))
    return jax.shard_map(
        per_device, mesh=mesh, in_specs=in_specs, out_specs=out_specs, check_vma=False
    )
```

```python
import functools

import jax
import jax.numpy as jnp
from jax import lax
from jax.experimental import pallas as pl
from jax.experimental.pallas import tpu as pltpu
from jax.sharding import PartitionSpec as P

DOUT = 1024
FF = 10944
ABLK = 1368

DAMPING = 0.1
CLIP_LEVEL = 0.5
MOMENTUM_RATE = 0.9
LEARN_RATE = 0.5

AXES = ("shard", "tensor")
ORDER = (0, 2, 3, 1)


def mirrored(position, j):
    return position + j * (len(ORDER) - 1 - 2 * position)


def route(shards, tensors, target):
    pairs = []
    for s in range(shards):
        for t in range(tensors):
            to = target(s, t)
            if to is not None:
                pairs.append((s * tensors + t, to[0] * tensors + to[1]))
    return pairs


def pick_transposed(tokens_t, where):
    hot = (where[None, :] == lax.broadcasted_iota(jnp.int32, (tokens_t.shape[1], where.shape[0]), 0))
    return jnp.dot(tokens_t, hot.astype(jnp.bfloat16), preferred_element_type=jnp.float32).astype(
        jnp.bfloat16
    )


def row_tiles(width, limit):
    count = -(-width // limit)
    size = -(-width // (count * 16)) * 16
    return [(at, min(size, width - at)) for at in range(0, width, size)]


def dot_nt(a, b):
    return lax.dot_general(a, b, (((1,), (1,)), ((), ())), preferred_element_type=jnp.float32)


def dot_nn(a, b):
    return jnp.dot(a, b, preferred_element_type=jnp.float32)


def damping_terms(trace, squares, width):
    shift = DAMPING * trace / width
    norm = jnp.sqrt(squares + 2.0 * shift * trace + width * shift * shift)
    return 1.0 / norm, shift / norm


def lay_out(parts, wide, chunks=None):
    at = 0
    for part in parts:
        lanes = part.shape[2]
        for i in range(part.shape[0]) if chunks is None else chunks:
            wide[:, at : at + lanes] = part[i]
            at += lanes


def gram_kernel(samples, *refs):
    *parts, gram, taken, wide = refs
    rows = taken.shape[1] // len(parts)
    for i, part in enumerate(parts):
        taken[:, i * rows : (i + 1) * rows] = part[samples]
    lay_out(parts, wide, range(samples))
    for at, size in row_tiles(gram.shape[0], 352):
        gram[at : at + size, :] = dot_nt(wide[at : at + size, :], wide[...])


def more_gram_kernel(samples, base, *refs):
    *parts, gram, wide = refs
    lay_out(parts, wide, range(samples))
    for at, size in row_tiles(gram.shape[0], 352):
        gram[at : at + size, :] = base[at : at + size, :] + dot_nt(wide[at : at + size, :], wide[...])


def factor_gram(wide, base, gram, scale):
    width = gram.shape[0]
    trace, squares = 0.0, 0.0
    for at, size in row_tiles(width, 352):
        tile = dot_nt(wide[at : at + size, :], wide[...])
        if base is not None:
            tile = tile + base[at : at + size, :]
        tile = tile * scale
        gram[at : at + size, :] = tile.astype(jnp.bfloat16)
        near = at // 128 * 128
        square = tile[:, near : at + size]
        row = lax.broadcasted_iota(jnp.int32, square.shape, 0) + (at - near)
        column = lax.broadcasted_iota(jnp.int32, square.shape, 1)
        trace = trace + jnp.sum(jnp.where(row == column, square, 0.0))
        squares = squares + jnp.sum(tile * tile)
    return trace, squares


def pick_kernel(upper, index, tokens, grad_rows, outer, inside):
    batches, _, count = tokens.shape
    picks = index.shape[1]

    def put(block, i, value):
        @pl.when(upper[0] == block)
        def _():
            outer[i] = value

        @pl.when(upper[0] != block)
        def _():
            inside[i] = value

    for i in range(batches):
        row = lax.broadcasted_iota(jnp.int32, (count, picks), 0)
        hot = (row == index[i : i + 1, :]).astype(jnp.float32).astype(jnp.bfloat16)
        chosen = dot_nn(tokens[i], hot)
        for block in range(2):
            put(block, i, chosen[block * ABLK : (block + 1) * ABLK].astype(jnp.bfloat16))
    rows = grad_rows[...].astype(jnp.float32)
    for block in range(2):
        put(block, batches, rows[block * ABLK : (block + 1) * ABLK].astype(jnp.bfloat16))


def grad_kernel(scale, rows, high, m, where, *refs):
    *q_parts, taken, poly, left, wide, gram = refs
    width = gram.shape[0]
    half = poly.shape[0]
    lay_out(q_parts, wide)
    trace, squares = factor_gram(wide, None, gram, scale)
    norm, shift = damping_terms(trace, squares, width)
    rounds = half // rows
    at = lax.broadcasted_iota(jnp.int32, (width, 128), 0)
    piece = at // rows
    arrival, other = piece % rounds, piece // rounds
    late, pair = arrival // (rounds // 2), arrival % (rounds // 2)
    turn = 2 * late + pair % 2
    position = sum(jnp.where(turn == i, p, 0) for i, p in enumerate(ORDER))
    low = 2 * (pair // 2) + (other ^ where[1])
    shard = mirrored(position, where[0]) * m + low
    place = (shard * rows + at % rows)[:, :1]
    hot = (place == lax.broadcasted_iota(jnp.int32, (width, width), 1)).astype(jnp.float32)
    hot = hot.astype(jnp.bfloat16)
    own = hot[:half]
    y1 = norm * dot_nn(own, gram[...]) + shift * own.astype(jnp.float32)
    y1_low = y1.astype(jnp.bfloat16)
    y2 = norm * dot_nn(y1_low, gram[...]) + shift * y1
    y2_low = y2.astype(jnp.bfloat16)
    y3 = norm * dot_nn(y2_low, gram[...]) + shift * y2
    total = (4.0 * y2 - 6.0 * y1 - y3).astype(jnp.bfloat16)
    poly[...] = dot_nt(total, hot).astype(jnp.bfloat16)
    on_time = taken.shape[1] // 2
    for at, size in row_tiles(left.shape[0], 352):
        own = taken[at : at + size, :on_time]
        mixed = dot_nt(own, poly[:, :on_time])
        mixed = mixed + dot_nt(taken[at : at + size, on_time:], poly[:, half : half + on_time])
        left[at : at + size, :on_time] = mixed[:, :on_time] + 4.0 * own.astype(jnp.float32)
        left[at : at + size, on_time:] = mixed[:, on_time:]


def act_kernel(scale, samples, update_rows, base, poly, early, taken, *refs):
    *refs, inner, all_rows, left, wide, gram, first, second, third = refs
    width, half = left.shape
    outs = half // update_rows
    parts, update = refs[:-outs], refs[-outs:]
    on_time = taken.shape[1] // 2
    for i in range(2):
        all_rows[:, i * half : i * half + on_time] = taken[:, i * on_time : (i + 1) * on_time]
        late = parts[i * len(parts) // 2 : (i + 1) * len(parts) // 2]
        rows = (half - on_time) // len(late)
        for k, part in enumerate(late):
            at = i * half + on_time + k * rows
            all_rows[:, at : at + rows] = part[samples][:, :rows]
    tiles = row_tiles(width, 352)
    for at, size in tiles:
        own = all_rows[at : at + size, on_time:half]
        mixed = early[at : at + size, :] + dot_nt(own, poly[:, on_time:half])
        mixed = mixed + dot_nt(all_rows[at : at + size, half + on_time :], poly[:, half + on_time :])
        left[at : at + size, :on_time] = mixed[:, :on_time].astype(jnp.bfloat16)
        mixed = mixed[:, on_time:] + 4.0 * own.astype(jnp.float32)
        left[at : at + size, on_time:] = mixed.astype(jnp.bfloat16)
    lay_out(parts[::2], wide, range(samples))
    trace, squares = factor_gram(wide, base, gram, scale)
    norm, shift = damping_terms(trace, squares, width)
    for at, size in tiles:
        rows = left[at : at + size, :].astype(jnp.float32)
        step = norm * dot_nn(gram[at : at + size, :], left[...]) + shift * rows
        step = 4.0 * rows - step
        first[at : at + size, :] = step
        second[at : at + size, :] = step.astype(jnp.bfloat16)
    total = 0.0
    for at, size in tiles:
        rows = left[at : at + size, :].astype(jnp.float32)
        step = norm * dot_nn(gram[at : at + size, :], second[...])
        step = step + shift * first[at : at + size, :] - 6.0 * rows
        first[at : at + size, :] = step
        third[at : at + size, :] = step.astype(jnp.bfloat16)
    for at, size in tiles:
        rows = left[at : at + size, :].astype(jnp.float32)
        step = norm * dot_nn(gram[at : at + size, :], third[...])
        done = step + shift * first[at : at + size, :] + 4.0 * rows
        total = total + jnp.sum(done * all_rows[at : at + size, :half].astype(jnp.float32))
        for k, out in enumerate(update):
            out[at : at + size, :] = done[:, k * update_rows : (k + 1) * update_rows].astype(jnp.bfloat16)
    inner[...] = jnp.full(inner.shape, total, jnp.float32)


def call(kernel, out_shape, scratch, operands, flops, vmem_mib, scalars=0):
    vmem = pl.BlockSpec(memory_space=pltpu.VMEM)
    smem = pl.BlockSpec(memory_space=pltpu.SMEM)
    moved = sum(x.size * x.dtype.itemsize for x in operands)
    return pl.pallas_call(
        kernel,
        out_shape=out_shape,
        in_specs=[smem] * scalars + [vmem] * (len(operands) - scalars),
        out_specs=jax.tree.map(lambda _: vmem, out_shape),
        scratch_shapes=[pltpu.VMEM(shape, dtype) for shape, dtype in scratch],
        compiler_params=pltpu.CompilerParams(vmem_limit_bytes=vmem_mib * 2**20),
        cost_estimate=pl.CostEstimate(flops=flops, bytes_accessed=moved, transcendentals=0),
    )(*operands)


def per_device(hidden_acts, out_grads, sample_idx, grad_weight, momentum, weight):
    n = lax.axis_size("shard")
    nt = lax.axis_size("tensor")
    batches, picks = sample_idx.shape
    rows, hidden = grad_weight.shape
    blocks = hidden // ABLK
    high = 2 * blocks
    m = n // high
    me = lax.axis_index("shard")
    col = lax.axis_index("tensor")
    core = col % 2
    hi = me // m
    lo = me % m

    def pairs_of(f):
        def target(s, t):
            to = f(s // m, s % m, t // 2, t % 2)
            return None if to is None else (to[0] * m + to[1], to[2] * 2 + to[3])

        return route(n, nt, target)

    def send(value, f, back=False):
        pairs = pairs_of(f)
        if back:
            pairs = [(to, source) for source, to in pairs]
        return lax.ppermute(value, AXES, pairs)

    def over_lo(value, d):
        return send(value, lambda h, l, y, c: (h, l ^ d, y, c))

    def over_core(value):
        return send(value, lambda h, l, y, c: (h, l, y, c ^ 1))

    def home(p):
        def target(h, l, y, c):
            j = 0 if h == ORDER[p % high] else 1
            if l // 2 != p // high or h != mirrored(ORDER[p % high], j):
                return None
            return (1 + j, c, y, l % 2)

        return target

    def outer_round(p):
        return p % high in (0, high - 1)

    upper = hi >= high // 2

    def after(value, others):
        return lax.optimization_barrier((value, others))[0]

    rounds = n // 2
    mine_j = hi - 1
    at_home = jnp.logical_and(jnp.logical_or(hi == 1, hi == 2), lo < 2)

    tokens_t = lax.dynamic_index_in_dim(out_grads, col // 2, 0, keepdims=False).T
    my_idx = lax.dynamic_index_in_dim(sample_idx, col // 2, 0, keepdims=False)
    q = pick_transposed(tokens_t, my_idx)
    q_own = [send(q, home(p)) for p in range(rounds)]
    bf16, f32 = jnp.bfloat16, jnp.float32
    assert rows == picks or n > 8
    grad_t = grad_weight.T
    if rows < picks:
        grad_t = jnp.pad(grad_t, ((0, 0), (0, picks - rows)))
    outer, inside = call(
        pick_kernel,
        (jax.ShapeDtypeStruct((batches + 1, ABLK, picks), bf16),) * 2,
        [],
        [upper.astype(jnp.int32).reshape(1), sample_idx, jnp.swapaxes(hidden_acts, 1, 2), grad_t],
        2 * batches * picks * hidden * hidden_acts.shape[1],
        vmem_mib=12,
        scalars=1,
    )
    late = [p for p in range(rounds) if p % high >= 2]
    early = [p for p in range(rounds) if p % high < 2]
    facing = lambda parts: [x for p, x in enumerate(parts) if p % high < 2]
    q_same = after(jnp.stack(q_own), [outer, inside])
    q_far = [
        send(q_same, lambda h, l, y, c, d=d: (h, l, y ^ d, c)) for d in range(1, nt // 2)
    ]
    turn = lambda p, pair: send(pair[0] if outer_round(p) else pair[1], home(p))
    on_time = [turn(p, (outer, inside)) for p in early]

    pair = after((outer, inside), [q_same])
    tardy = [turn(p, pair) for p in late]
    on_time_other = [over_core(x) for x in on_time]
    q_parts = [q_same] + q_far
    q_parts = q_parts + [over_core(x) for x in q_parts]

    count = batches * picks * n
    scale = 1.0 / count
    half = rounds * rows
    where = jnp.stack([mine_j & 1, core]).astype(jnp.int32)
    share = len(early) / rounds
    base, taken = call(
        functools.partial(gram_kernel, batches),
        (
            jax.ShapeDtypeStruct((ABLK, ABLK), f32),
            jax.ShapeDtypeStruct((ABLK, 2 * len(early) * picks), bf16),
        ),
        [((ABLK, int(count * share)), bf16)],
        on_time + on_time_other,
        int(2 * ABLK * ABLK * count * share),
        vmem_mib=12 if n == 8 else 40,
    )
    if rows < picks:
        taken = taken.reshape(ABLK, -1, picks)[:, :, :rows].reshape(ABLK, -1)
    poly, left_early = call(
        functools.partial(grad_kernel, scale, rows, high, m),
        (jax.ShapeDtypeStruct((half, DOUT), bf16), jax.ShapeDtypeStruct((ABLK, half), f32)),
        [((DOUT, count), bf16), ((DOUT, DOUT), bf16)],
        [where, *q_parts, taken],
        2 * DOUT * (DOUT * count + 4 * half * DOUT + ABLK * half // 2),
        vmem_mib=28 if n == 8 else 58,
        scalars=1,
    )

    local = [after(x, poly) for x, p in zip(tardy, late) if p % high == 3]
    local = [(x, over_core(x)) for x in local]
    last = [x for x, p in zip(tardy, late) if p % high == 2]
    last = after(last, [poly, base] + last)
    base = after(base, last)
    last = [(x, over_core(x)) for x in last]
    base = call(
        functools.partial(more_gram_kernel, batches),
        jax.ShapeDtypeStruct((ABLK, ABLK), f32),
        [((ABLK, count // 4), bf16)],
        [base] + [x for x, _ in local] + [x for _, x in local],
        2 * ABLK * ABLK * count // 4,
        vmem_mib=12 if n == 8 else 30,
    )
    tardy = [pair[i] for i in range(2) for both in zip(last, local) for pair in both]
    piece = rows if rows % 128 == 0 else half
    *update, inner = call(
        functools.partial(act_kernel, scale, batches, piece),
        (jax.ShapeDtypeStruct((ABLK, piece), bf16),) * (half // piece)
        + (jax.ShapeDtypeStruct((8, 128), f32),),
        [
            ((ABLK, DOUT), bf16),
            ((ABLK, half), bf16),
            ((ABLK, count // 4), bf16),
            ((ABLK, ABLK), bf16),
            ((ABLK, half), f32),
            ((ABLK, half), bf16),
            ((ABLK, half), bf16),
        ],
        [base, poly, left_early, taken] + tardy,
        int(2 * ABLK * (ABLK * (count // 4 + 3 * half) + half * DOUT // 2)),
        vmem_mib=28 if n == 8 else 46,
    )

    back = [
        send(update[a * rows // piece][:, a * rows % piece :][:, :rows], home(p), back=True)
        for p, a in sorted((p, a) for a, p in enumerate(early + late))
    ]
    mine = jnp.where(at_home, inner[:1], 0.0)
    heard = lax.all_to_all(jnp.broadcast_to(mine[None], (n * nt, 1, 128)), AXES, 0, 0)
    total = jnp.sum(heard, axis=0)
    ratio = jnp.minimum(1.0, CLIP_LEVEL / jnp.sqrt(total[0, 0] / (DOUT * FF)))

    got_outer = sum(x.astype(f32) for p, x in reversed(list(enumerate(back))) if outer_round(p))
    got_inside = sum(x.astype(f32) for p, x in reversed(list(enumerate(back))) if not outer_round(p))
    final = jnp.concatenate(
        [jnp.where(upper, got_inside, got_outer), jnp.where(upper, got_outer, got_inside)], axis=0
    )
    new_momentum = MOMENTUM_RATE * momentum.T + ratio * final
    new_weight = weight.T - LEARN_RATE * new_momentum
    return (new_momentum.T, new_weight.T)


def solution(mesh):
    in_specs = (
        P(None, "shard", "tensor"),
        P(None, "shard", None),
        P(None, "shard"),
        P("shard", "tensor"),
        P("shard", "tensor"),
        P("shard", "tensor"),
    )
    out_specs = (P("shard", "tensor"), P("shard", "tensor"))
    return jax.shard_map(
        per_device, mesh=mesh, in_specs=in_specs, out_specs=out_specs, check_vma=False
    )
```
